128 devices in a mesh: row: 8 (over z, core), col: 16 (over y, x).
Axes of the slice: x: 4, y: 4, z: 4, core: 2. Of those that a mesh axis runs over, the one named last changes fastest.
Arguments:
- front_matrix: float32 [12288, 12288], P('row', 'col')
- child_tiles: float32 [16384, 256, 128], P(('row', 'col')), may hold values from -0.25 to 0.25
- owner_index: int32 [16384], P(('row', 'col')), may hold values from 0 to 127, as said below
- slot_index: int32 [16384], P(('row', 'col')), may hold values from 0 to 35, as said below
Outputs:
- updated_front: float32 [12288, 12288], P('row', 'col')
The draws below stay inside these ranges and needn't reach their ends.
Inputs may be any that keep to these rules, and one draw needn't show every extreme that they name: `owner_index`: each device's 128 blocks name at most 2 blocks for any one owner, and every device sends exactly 2 to some common owner. `slot_index`: blocks for owner 0 never land in its first 512 rows.
All inputs are finite; a program needn't handle non-finite values.
Results may differ from the reference program's by a relative error of at most 0.0003.
Values sent between devices are 32-bit elements; how exact they have to be, the bound alone decides.
A program may use at most 192 MiB of HBM per device.

```python
import jax
import jax.numpy as jnp
from jax import lax

F = 12288
P_SIZE = 512
TR = 256
TC = 128
CT_DEV = 128
OWNERS = 128
CAP = 2
RL = 1536
TRN = 6
TCN = 6
LT = 36
N_ROW = 8
N_COL = 16


def route_table(key):
    key_hot, key_perm, key_mix = jax.random.split(key, 3)
    hot_owner = jax.random.randint(key_hot, (), 0, OWNERS)

    def source_row(source):
        ordering = jax.random.permutation(jax.random.fold_in(key_perm, source), OWNERS)
        first_owner = ordering[0]
        ordering = jnp.where(ordering == hot_owner, first_owner, ordering).at[0].set(hot_owner)
        picked = ordering[jnp.arange(CT_DEV) // CAP]
        shuffle = jax.random.permutation(jax.random.fold_in(key_mix, source), CT_DEV)
        return picked[shuffle]
    return jax.vmap(source_row)(jnp.arange(OWNERS)).reshape(-1).astype(jnp.int32)


def draw_owner_index(key, part):
    return route_table(key)


def draw_slot_index(key, part):
    owners = route_table(key)
    key = jax.random.fold_in(key, 7)
    raw_slot = jax.random.randint(key, (OWNERS * CT_DEV,), 0, LT)
    lowest = P_SIZE // TR * TCN
    shifted = lowest + raw_slot % (LT - lowest)
    return jnp.where(owners == 0, shifted, raw_slot).astype(jnp.int32)


def draw_front_matrix(key, part):
    key = jax.random.fold_in(key, 11)
    key_base, key_couple = jax.random.split(key, 2)
    values_base = jax.random.uniform(key_base, (F, F), jnp.float32, -1.0, 1.0)
    coupling = jax.random.normal(key_couple, (P_SIZE, P_SIZE), jnp.float32)
    gram = jnp.dot(coupling, coupling.T, precision=lax.Precision.HIGHEST) / P_SIZE
    diagonal_block = gram + jnp.eye(P_SIZE, dtype=jnp.float32)
    global_col = lax.broadcasted_iota(jnp.int32, (F, F), 1)
    region_scale = jnp.where(global_col < P_SIZE, 0.3, 1.0)
    values = values_base * region_scale
    return values.at[:P_SIZE, :P_SIZE].set(diagonal_block).astype(jnp.float32)


def shard_levels(stream_key, extent, pieces, low, largest):
    factor_of = 1.0
    for position, blocks in pieces:
        draws = jax.random.uniform(jax.random.fold_in(jax.random.fold_in(stream_key, 6), position), (blocks,), jnp.float32, low / len(pieces), largest / len(pieces))
        factor_of = factor_of * jnp.repeat(jnp.exp(draws), extent[position] // blocks).reshape((-1,) + (1,) * (len(extent) - 1 - position))
    return factor_of


def setup_inputs(seed: int = 0) -> dict:
    splits = jax.random.split(jax.random.key(seed), 5)
    return {
        "front_matrix": draw_front_matrix(jax.random.fold_in(splits[4], 71), 0),
        "child_tiles": jnp.clip(jax.random.uniform(splits[1], (OWNERS * CT_DEV, TR, TC), jnp.float32, -0.25, 0.25) * shard_levels(splits[1], (OWNERS * CT_DEV, TR, TC), ((0, 128),), -0.4, 0.0), -0.25, 0.25),
        "owner_index": draw_owner_index(jax.random.fold_in(splits[4], 71), 0),
        "slot_index": draw_slot_index(jax.random.fold_in(splits[4], 71), 0),
    }


def factor_block(block):
    factor = jnp.linalg.cholesky(0.5 * (block + block.T))
    identity = jnp.eye(block.shape[0], dtype=block.dtype)
    inverse = jax.scipy.linalg.solve_triangular(factor, identity, lower=True)
    return (jnp.tril(factor), inverse)

def reference(front_matrix, child_tiles, owner_index, slot_index):
    grid_row = owner_index // N_COL
    grid_col = owner_index % N_COL
    block_row = grid_row * TRN + slot_index // TCN
    block_col = grid_col * TCN + slot_index % TCN
    blocks = front_matrix.reshape(F // TR, TR, F // TC, TC)
    blocks = blocks.at[block_row, :, block_col, :].add(child_tiles)
    assembled = blocks.reshape(F, F)
    factor, inverse = factor_block(assembled[:P_SIZE, :P_SIZE])
    panel_cols = jnp.dot(assembled[:, :P_SIZE], inverse.T, precision=lax.Precision.HIGHEST, preferred_element_type=assembled.dtype)
    panel_cols = panel_cols.at[:P_SIZE].set(factor)

    def row_block(block_index):
        row_start = block_index * RL
        rows_here = lax.dynamic_slice_in_dim(assembled, row_start, RL, 0)
        panel_rows = lax.dynamic_slice_in_dim(panel_cols, row_start, RL, 0)
        update = jnp.dot(panel_rows, panel_cols.T, precision=lax.Precision.HIGHEST, preferred_element_type=assembled.dtype)
        global_row = row_start + lax.broadcasted_iota(jnp.int32, (RL, F), 0)
        global_col = lax.broadcasted_iota(jnp.int32, (RL, F), 1)
        result = jnp.where(global_row >= global_col, rows_here - update, rows_here)
        panel_wide = jnp.concatenate([panel_rows, jnp.zeros((RL, F - P_SIZE), assembled.dtype)], 1)
        return jnp.where(global_col < P_SIZE, panel_wide, result)
    updated = lax.map(row_block, jnp.arange(N_ROW, dtype=jnp.int32))
    return updated.reshape(F, F)
```

```python
import functools

import jax
import jax.numpy as jnp
from jax import lax
from jax.experimental import pallas as pl
from jax.experimental.pallas import tpu as pltpu
from jax.sharding import PartitionSpec as P

P_SIZE = 512
MESH = pl.DeviceIdType.MESH
ROWS = (88, 88, 80)
STARTS = (0, 88, 176)
HALF = (40, 40, 40)
ORDERS = ("zxy", "xyz", "yzx")
SHIFTS = (2, 1, 3, 0)
SLOTS = 36


def position():
    row = lax.axis_index("row")
    col = lax.axis_index("col")
    return {"z": row // 2, "k": lax.rem(row, 2), "y": col // 4, "x": lax.rem(col, 4)}


def device(at):
    return (at["z"] * 2 + at["k"], at["y"] * 4 + at["x"])


def moved(at, **steps):
    to = dict(at)
    for name, step in steps.items():
        to[name] = lax.rem(at[name] + step, 2 if name == "k" else 4)
    return to


def exchange_kernel(
    where_ref, prev_ref, last_ref, child, front, out, arr0, arr1, arr2, mid0, mid1, mid2, *scratch
):
    arrived = (arr0, arr1, arr2)
    middle = (mid0, mid1, mid2)
    staging, got = scratch[0:3], scratch[3:6]
    far, right, left = scratch[6:9], scratch[9:12], scratch[12:15]
    in_far, in_left, in_right = scratch[15:18], scratch[18:21], scratch[21:24]
    send_a, recv_a, send_b, recv_b, send_c, recv_c, load_sem, front_sem, out_sem = scratch[24:]
    me = position()

    barrier = pltpu.get_barrier_semaphore()
    partners = [moved(me, k=1)]
    for axis in "zyx":
        for step in (1, 2, 3):
            for core in (0, 1):
                partners.append(moved(me, **{axis: step, "k": core}))
    for to in partners:
        pl.semaphore_signal(barrier, inc=1, device_id=device(to), device_id_type=MESH)

    def pack(t, p):
        d, e, f = ORDERS[p]
        shift = SHIFTS[t]

        def body(i, carry):
            at = {
                d: i // 16,
                "k": lax.rem(i // 8, 2),
                e: lax.rem(i // 2, 4),
                f: lax.rem(me[f] + shift, 4),
            }
            owner = ((at["z"] * 2 + at["k"]) * 4 + at["y"]) * 4 + at["x"]
            index = where_ref[owner * 2 + lax.rem(i, 2)]
            staging[p][i // 8, lax.rem(i // 2, 4), lax.rem(i, 2)] = child[
                index, STARTS[p] : STARTS[p] + ROWS[p], :
            ]
            return carry

        lax.fori_loop(0, 64, body, 0)

    def group(at, d):
        return at[d] * 2 + at["k"]

    def start_a(t, p):
        d = ORDERS[p][0]
        mine = group(me, d)
        for step, core in ((1, 0), (3, 0), (1, 1), (3, 1), (2, 0), (2, 1), (0, 1)):
            to = moved(me, **{d: step, "k": core})
            pltpu.make_async_remote_copy(
                src_ref=staging[p].at[group(to, d)],
                dst_ref=arrived[p].at[t, :, mine],
                send_sem=send_a.at[t, p],
                recv_sem=recv_a.at[t, p],
                device_id=device(to),
                device_id_type=MESH,
            ).start()
        pltpu.make_async_copy(
            staging[p].at[mine], arrived[p].at[t, :, mine], recv_a.at[t, p]
        ).start()

    def wait_send_a(t, p):
        part = staging[p].at[pl.ds(0, 7)]
        pltpu.make_async_copy(part, part, send_a.at[t, p]).wait()

    def start_b(t, p):
        e = ORDERS[p][1]
        whole = arrived[p].at[t]
        pltpu.make_async_copy(whole, whole, recv_a.at[t, p]).wait()
        for step in (1, 3, 2):
            to = moved(me, **{e: step})
            pltpu.make_async_remote_copy(
                src_ref=arrived[p].at[t, to[e]],
                dst_ref=middle[p].at[t, me[e]],
                send_sem=send_b.at[t, p],
                recv_sem=recv_b.at[t, p],
                device_id=device(to),
                device_id_type=MESH,
            ).start()
        pltpu.make_async_copy(
            arrived[p].at[t, me[e]], middle[p].at[t, me[e]], recv_b.at[t, p]
        ).start()

    def load(t, p):
        whole = middle[p].at[t]
        pltpu.make_async_copy(whole, whole, recv_b.at[t, p]).wait()
        pltpu.make_async_copy(whole, got[p].at[pl.ds(0, 4)], load_sem.at[p]).start()

    def to_neighbour(source, target, p, kind, step):
        f = ORDERS[p][2]
        return pltpu.make_async_remote_copy(
            src_ref=source,
            dst_ref=target,
            send_sem=send_c.at[kind, p],
            recv_sem=recv_c.at[kind, p],
            device_id=device(moved(me, **{f: step})),
            device_id_type=MESH,
        )

    def far_copies(p):
        low, high = pl.ds(0, HALF[p]), pl.ds(HALF[p], ROWS[p] - HALF[p])
        return (
            to_neighbour(far[p].at[:, low], in_far[p].at[:, low], p, 0, 1),
            to_neighbour(far[p].at[:, high], in_far[p].at[:, high], p, 1, 3),
        )

    def front_copy(p, q):
        rows = pl.ds(q // 6 * 256 + STARTS[p], ROWS[p])
        return front.at[rows, pl.ds(q % 6 * 128, 128)], far[p].at[q], front_sem.at[p]

    def out_copy(p, q):
        rows = pl.ds(q // 6 * 256 + STARTS[p], ROWS[p])
        return far[p].at[q], out.at[rows, pl.ds(q % 6 * 128, 128)], out_sem.at[p]

    def add_up(t, p):
        rows = ROWS[p]
        held = got[p]
        pltpu.make_async_copy(
            middle[p].at[t], held.at[pl.ds(0, 4)], load_sem.at[p]
        ).wait()

        def at(k):
            return k // 16, lax.rem(k // 2, 8), lax.rem(k, 2)

        def chain(k, carry):
            to = at(k)
            held[to] = held[to] + held[at(prev_ref[(p * 4 + t) * 64 + k])]
            return carry

        lax.fori_loop(0, 64, chain, 0)

        def total(q):
            return held[at(last_ref[(p * 4 + t) * SLOTS + q])]

        half = HALF[p]
        shift = SHIFTS[t]
        if shift == 2:

            def body(q, carry):
                far[p][q] = total(q)
                return carry

            lax.fori_loop(0, SLOTS, body, 0)
            for copy in far_copies(p):
                copy.start()
        elif shift == 1:
            far_copies(p)[0].wait_recv()

            def body(q, carry):
                right[p][q] = total(q)
                right[p][q, 0:half] = right[p][q, 0:half] + in_far[p][q, 0:half]
                return carry

            lax.fori_loop(0, SLOTS, body, 0)
            to_neighbour(right[p], in_left[p], p, 2, 1).start()
        elif shift == 3:
            far_copies(p)[1].wait_recv()

            def body(q, carry):
                left[p][q] = total(q)
                left[p][q, half:rows] = left[p][q, half:rows] + in_far[p][q, half:rows]
                return carry

            lax.fori_loop(0, SLOTS, body, 0)
            to_neighbour(left[p], in_right[p], p, 3, 3).start()
            for copy in far_copies(p):
                copy.wait_send()
            for q in range(SLOTS):
                pltpu.make_async_copy(*front_copy(p, q)).start()
        else:
            whole = far[p]
            pltpu.make_async_copy(whole, whole, front_sem.at[p]).wait()

            def own(q, carry):
                far[p][q] = far[p][q] + total(q)
                return carry

            lax.fori_loop(0, SLOTS, own, 0)
            to_neighbour(right[p], in_left[p], p, 2, 1).wait()
            to_neighbour(left[p], in_right[p], p, 3, 3).wait()

            def body(q, carry):
                far[p][q] = far[p][q] + in_left[p][q] + in_right[p][q]
                return carry

            lax.fori_loop(0, SLOTS, body, 0)
            for q in range(SLOTS):
                pltpu.make_async_copy(*out_copy(p, q)).start()

    for p in range(3):
        pack(0, p)
        got[p][4] = jnp.zeros((8, 2, ROWS[p], 128), jnp.float32)
    pl.semaphore_wait(barrier, len(partners))
    for p in range(3):
        start_a(0, p)
    for t in range(4):
        for p in range(3):
            start_b(t, p)
            if t + 1 < 4:
                wait_send_a(t, p)
                pack(t + 1, p)
                start_a(t + 1, p)
        if t > 0:
            for p in range(3):
                load(t - 1, p)
            for p in range(3):
                add_up(t - 1, p)
    for p in range(3):
        load(3, p)
    for p in range(3):
        add_up(3, p)
    for p in range(3):
        wait_send_a(3, p)
        for t in range(4):
            part = middle[p].at[t, pl.ds(0, 3)]
            pltpu.make_async_copy(part, part, send_b.at[t, p]).wait()
        whole = far[p]
        pltpu.make_async_copy(whole, whole, out_sem.at[p]).wait()


def exchange(where, prev, last, child_tiles, front_matrix):
    f32 = jnp.float32
    scratch = [pltpu.VMEM((8, 4, 2, r, 128), f32) for r in ROWS]
    scratch += [pltpu.VMEM((5, 8, 2, r, 128), f32) for r in ROWS]
    for _ in range(6):
        scratch += [pltpu.VMEM((SLOTS, r, 128), f32) for r in ROWS]
    scratch += [pltpu.SemaphoreType.DMA((4, 3))] * 6
    scratch += [pltpu.SemaphoreType.DMA((3,))] * 3
    anywhere = pl.BlockSpec(memory_space=pl.ANY)
    outs = [jax.ShapeDtypeStruct(front_matrix.shape, f32)]
    outs += [jax.ShapeDtypeStruct((4, 4, 8, 2, r, 128), f32) for r in ROWS]
    outs += [jax.ShapeDtypeStruct((4, 4, 8, 2, r, 128), f32) for r in ROWS]
    return pl.pallas_call(
        exchange_kernel,
        out_shape=outs,
        in_specs=[pl.BlockSpec(memory_space=pltpu.SMEM)] * 3
        + [pl.BlockSpec(memory_space=pltpu.VMEM), anywhere],
        out_specs=[anywhere] * 7,
        scratch_shapes=scratch,
        compiler_params=pltpu.CompilerParams(
            collective_id=1, has_side_effects=True, vmem_limit_bytes=62 << 20
        ),
        name="exchange",
    )(where, prev, last, child_tiles, front_matrix)[0]


def routing(owner_index, slot_index):
    count = owner_index.shape[0]
    item = lax.broadcasted_iota(jnp.int32, (count, count), 0)
    other = lax.broadcasted_iota(jnp.int32, (count, count), 1)
    same = (owner_index[:, None] == owner_index[None, :]) & (item > other)
    place = owner_index * 2 + jnp.sum(same.astype(jnp.int32), axis=1)
    hit = place[:, None] == lax.broadcasted_iota(jnp.int32, (count, 256), 1)
    where = jnp.sum(jnp.where(hit, lax.broadcasted_iota(jnp.int32, hit.shape, 0), 0), axis=0)
    slots = jnp.sum(jnp.where(hit, slot_index[:, None] + 1, 0), axis=0) - 1
    table = lax.all_gather(slots.astype(jnp.float32), ("row", "col"))
    me = position()
    pick_source, pick_owner = [], []
    source = jnp.arange(128)
    source = {"z": source // 32, "k": source // 16 % 2, "y": source // 4 % 4, "x": source % 4}
    place = jnp.arange(256)
    target = {"z": place // 64, "k": place // 32 % 2, "y": place // 8 % 4, "x": place // 2 % 4}
    for p in range(3):
        d, e, f = ORDERS[p]
        r = jnp.arange(32)
        pick_source.append(
            (source[e][None] == (r // 8)[:, None])
            & (source[d][None] == (r // 2 % 4)[:, None])
            & (source["k"][None] == (r % 2)[:, None])
            & (source[f] == me[f])[None]
        )
        n = jnp.arange(8)
        shift = jnp.array(SHIFTS)[n // 2]
        pick_owner.append(
            (target[d] == me[d])[:, None]
            & (target["k"] == me["k"])[:, None]
            & (target[e] == me[e])[:, None]
            & (target[f][:, None] == ((me[f] + shift) % 4)[None])
            & ((place % 2)[:, None] == (n % 2)[None])
        )
    rows = jnp.dot(
        jnp.concatenate(pick_source, 0).astype(jnp.float32),
        table,
        precision=lax.Precision.HIGHEST,
    )
    entries = jnp.stack(
        [
            jnp.dot(rows[p * 32 : p * 32 + 32], pick_owner[p].astype(jnp.float32))
            for p in range(3)
        ]
    )
    entries = entries.reshape(3, 32, 4, 2).transpose(0, 2, 1, 3).reshape(12, 64)
    entries = jnp.round(entries).astype(jnp.int32)
    k = lax.broadcasted_iota(jnp.int32, (12, 64, 64), 1)
    j = lax.broadcasted_iota(jnp.int32, (12, 64, 64), 2)
    match = (entries[:, :, None] == entries[:, None, :]) & (entries[:, :, None] >= 0) & (j < k)
    prev = jnp.max(jnp.where(match, j, -1), axis=2)
    prev = jnp.where(prev < 0, 64, prev)
    q = lax.broadcasted_iota(jnp.int32, (12, SLOTS, 64), 1)
    j = lax.broadcasted_iota(jnp.int32, (12, SLOTS, 64), 2)
    last = jnp.max(jnp.where(entries[:, None, :] == q, j, -1), axis=2)
    last = jnp.where(last < 0, 64, last)
    return where, prev.reshape(-1), last.reshape(-1)


def assemble(front_matrix, child_tiles, owner_index, slot_index):
    where, prev, last = routing(owner_index, slot_index)
    return exchange(where, prev, last, child_tiles, front_matrix)


def spread(block, axis, source):
    block = jnp.where(lax.axis_index(axis) == source, block, jnp.zeros_like(block))
    return lax.psum(block, axis)


def factor_block(block):
    factor = jnp.linalg.cholesky(0.5 * (block + block.T))
    identity = jnp.eye(block.shape[0], dtype=jnp.float32)
    inverse = jax.scipy.linalg.solve_triangular(factor, identity, lower=True)
    return (jnp.tril(factor), inverse)


def solve_panel(columns, factor, inverse, row_start):
    solved = lax.dot_general(
        columns,
        inverse,
        (((1,), (1,)), ((), ())),
        precision=lax.Precision.HIGHEST,
        preferred_element_type=jnp.float32,
    )
    panel_size = factor.shape[0]
    padded = jnp.concatenate(
        [factor, jnp.zeros((columns.shape[0] - panel_size, panel_size), jnp.float32)], 0
    )
    global_row = row_start + lax.broadcasted_iota(jnp.int32, solved.shape, 0)
    return jnp.where(global_row < panel_size, padded, solved)


def local(front_matrix, child_tiles, owner_index, slot_index):
    rows_loc, cols_loc = front_matrix.shape
    assembled = assemble(front_matrix, child_tiles, owner_index, slot_index)
    my_row = lax.axis_index("row")
    my_col = lax.axis_index("col")
    row_start = my_row * rows_loc
    diagonal = spread(assembled[:P_SIZE, :P_SIZE], "row", 0)
    diagonal = jnp.where(my_col == 0, diagonal, jnp.eye(P_SIZE, dtype=jnp.float32))
    factor, inverse = factor_block(diagonal)
    own_panel = solve_panel(assembled[:, :P_SIZE], factor, inverse, row_start)
    panel_rows = spread(own_panel, "col", 0)
    offset = my_col * cols_loc % rows_loc
    root_row = my_col * cols_loc // rows_loc
    column_piece = lax.dynamic_slice_in_dim(panel_rows, offset, cols_loc, 0)
    column_rows = spread(column_piece, "row", root_row)
    update = lax.dot_general(
        panel_rows,
        column_rows,
        (((1,), (1,)), ((), ())),
        precision=lax.Precision.HIGHEST,
        preferred_element_type=jnp.float32,
    )
    global_row = row_start + lax.broadcasted_iota(jnp.int32, (rows_loc, cols_loc), 0)
    global_col = my_col * cols_loc + lax.broadcasted_iota(jnp.int32, (rows_loc, cols_loc), 1)
    lowered = jnp.where(global_row >= global_col, assembled - update, assembled)
    panel_wide = jnp.concatenate(
        [panel_rows, jnp.zeros((rows_loc, cols_loc - P_SIZE), jnp.float32)], 1
    )
    return jnp.where(global_col < P_SIZE, panel_wide, lowered)


def solution(mesh):
    placed = (P("row", "col"), P(("row", "col"), None, None), P(("row", "col")), P(("row", "col")))
    return jax.shard_map(
        local, mesh=mesh, in_specs=placed, out_specs=P("row", "col"), check_vma=False
    )
```

```python
import functools

import jax
import jax.numpy as jnp
from jax import lax
from jax.experimental import pallas as pl
from jax.experimental.pallas import tpu as pltpu
from jax.sharding import PartitionSpec as P

P_SIZE = 512
MESH = pl.DeviceIdType.MESH
ROWS = (88, 88, 80)
STARTS = (0, 88, 176)
HALF = (40, 40, 40)
ORDERS = ("zxy", "xyz", "yzx")
SHIFTS = (2, 1, 3, 0)
SLOTS = 36
BANDS = ((0, 256, 256), (256, 128, 384), (384, 128, 512))


def position():
    row = lax.axis_index("row")
    col = lax.axis_index("col")
    return {"z": row // 2, "k": lax.rem(row, 2), "y": col // 4, "x": lax.rem(col, 4)}


def device(at):
    return (at["z"] * 2 + at["k"], at["y"] * 4 + at["x"])


def moved(at, **steps):
    to = dict(at)
    for name, step in steps.items():
        to[name] = lax.rem(at[name] + step, 2 if name == "k" else 4)
    return to


def exchange_kernel(
    where_ref,
    prev_ref,
    last_ref,
    child,
    front,
    out,
    arr0,
    arr1,
    arr2,
    mid0,
    mid1,
    mid2,
    square,
    factor_out,
    *scratch,
):
    arrived = (arr0, arr1, arr2)
    middle = (mid0, mid1, mid2)
    staging, pools = scratch[0:3], scratch[3:5]
    got = [pools[p % 2].at[:, pl.ds(0, ROWS[p])] for p in range(3)]
    far, right, left = scratch[5:8], scratch[8:11], scratch[11:14]
    in_far, in_left, in_right = scratch[14:17], scratch[17:20], scratch[20:23]
    send_a, recv_a, send_b, recv_b, send_c, recv_c, load_sem, front_sem, out_sem = scratch[23:32]
    send_s, recv_s, corner_sem, work, inverse = scratch[32:]
    me = position()

    barrier = pltpu.get_barrier_semaphore()
    partners = [moved(me, k=1)]
    for axis in "zyx":
        for step in (1, 2, 3):
            for core in (0, 1):
                partners.append(moved(me, **{axis: step, "k": core}))
    for to in partners:
        pl.semaphore_signal(barrier, inc=1, device_id=device(to), device_id_type=MESH)

    def pack(t, p):
        d, e, f = ORDERS[p]
        shift = SHIFTS[t]

        def body(i, carry):
            at = {
                d: i // 16,
                "k": lax.rem(i // 8, 2),
                e: lax.rem(i // 2, 4),
                f: lax.rem(me[f] + shift, 4),
            }
            owner = ((at["z"] * 2 + at["k"]) * 4 + at["y"]) * 4 + at["x"]
            index = where_ref[owner * 2 + lax.rem(i, 2)]
            staging[p][i // 8, lax.rem(i // 2, 4), lax.rem(i, 2)] = child[
                index, STARTS[p] : STARTS[p] + ROWS[p], :
            ]
            return carry

        lax.fori_loop(0, 64, body, 0)

    def group(at, d):
        return at[d] * 2 + at["k"]

    def start_a(t, p):
        d = ORDERS[p][0]
        mine = group(me, d)
        for step, core in ((1, 0), (3, 0), (1, 1), (3, 1), (2, 0), (2, 1), (0, 1)):
            to = moved(me, **{d: step, "k": core})
            pltpu.make_async_remote_copy(
                src_ref=staging[p].at[group(to, d)],
                dst_ref=arrived[p].at[t, :, pl.ds(mine * 2, 2)],
                send_sem=send_a.at[t, p],
                recv_sem=recv_a.at[t, p],
                device_id=device(to),
                device_id_type=MESH,
            ).start()
        pltpu.make_async_copy(
            staging[p].at[mine], arrived[p].at[t, :, pl.ds(mine * 2, 2)], recv_a.at[t, p]
        ).start()

    def wait_send_a(t, p):
        part = staging[p].at[pl.ds(0, 7)]
        pltpu.make_async_copy(part, part, send_a.at[t, p]).wait()

    def start_b(t, p):
        e = ORDERS[p][1]
        whole = arrived[p].at[t]
        pltpu.make_async_copy(whole, whole, recv_a.at[t, p]).wait()
        for step in (1, 3, 2):
            to = moved(me, **{e: step})
            pltpu.make_async_remote_copy(
                src_ref=arrived[p].at[t, to[e]],
                dst_ref=middle[p].at[t, pl.ds(me[e] * 16, 16)],
                send_sem=send_b.at[t, p],
                recv_sem=recv_b.at[t, p],
                device_id=device(to),
                device_id_type=MESH,
            ).start()
        pltpu.make_async_copy(
            arrived[p].at[t, me[e]], middle[p].at[t, pl.ds(me[e] * 16, 16)], recv_b.at[t, p]
        ).start()

    def load(t, p):
        whole = middle[p].at[t]
        pltpu.make_async_copy(whole, whole, recv_b.at[t, p]).wait()
        pltpu.make_async_copy(whole, got[p].at[pl.ds(0, 64)], load_sem.at[p]).start()

    def to_neighbour(source, target, p, kind, step):
        f = ORDERS[p][2]
        return pltpu.make_async_remote_copy(
            src_ref=source,
            dst_ref=target,
            send_sem=send_c.at[kind, p],
            recv_sem=recv_c.at[kind, p],
            device_id=device(moved(me, **{f: step})),
            device_id_type=MESH,
        )

    def far_copies(p):
        low, high = pl.ds(0, HALF[p]), pl.ds(HALF[p], ROWS[p] - HALF[p])
        return (
            to_neighbour(far[p].at[:, low], in_far[p].at[:, low], p, 0, 1),
            to_neighbour(far[p].at[:, high], in_far[p].at[:, high], p, 1, 3),
        )

    def front_copy(p, q):
        rows = pl.ds(q // 6 * 256 + STARTS[p], ROWS[p])
        return front.at[rows, pl.ds(q % 6 * 128, 128)], far[p].at[q], front_sem.at[p]

    def out_copy(p, q):
        rows = pl.ds(q // 6 * 256 + STARTS[p], ROWS[p])
        return far[p].at[q], out.at[rows, pl.ds(q % 6 * 128, 128)], out_sem.at[p]

    def add_up(t, p):
        rows = ROWS[p]
        held = got[p]
        pltpu.make_async_copy(
            middle[p].at[t], held.at[pl.ds(0, 64)], load_sem.at[p]
        ).wait()

        def chain(k, carry):
            held[k] = held[k] + held[prev_ref[(p * 4 + t) * 64 + k]]
            return carry

        lax.fori_loop(0, 64, chain, 0)

        def total(q):
            return held[last_ref[(p * 4 + t) * SLOTS + q]]

        half = HALF[p]
        shift = SHIFTS[t]
        if shift == 2:

            def body(q, carry):
                far[p][q] = total(q)
                return carry

            lax.fori_loop(0, SLOTS, body, 0)
            for copy in far_copies(p):
                copy.start()
        elif shift == 1:
            far_copies(p)[0].wait_recv()

            def body(q, carry):
                right[p][q] = total(q)
                right[p][q, 0:half] = right[p][q, 0:half] + in_far[p][q, 0:half]
                return carry

            lax.fori_loop(0, SLOTS, body, 0)
            to_neighbour(right[p], in_left[p], p, 2, 1).start()
        elif shift == 3:
            far_copies(p)[1].wait_recv()

            def body(q, carry):
                left[p][q] = total(q)
                left[p][q, half:rows] = left[p][q, half:rows] + in_far[p][q, half:rows]
                return carry

            lax.fori_loop(0, SLOTS, body, 0)
            to_neighbour(left[p], in_right[p], p, 3, 3).start()
            for copy in far_copies(p):
                copy.wait_send()
            for q in range(SLOTS):
                pltpu.make_async_copy(*front_copy(p, q)).start()
        else:
            whole = far[p]
            pltpu.make_async_copy(whole, whole, front_sem.at[p]).wait()

            def own(q, carry):
                far[p][q] = far[p][q] + total(q)
                return carry

            lax.fori_loop(0, SLOTS, own, 0)
            to_neighbour(right[p], in_left[p], p, 2, 1).wait()
            to_neighbour(left[p], in_right[p], p, 3, 3).wait()

            def body(q, carry):
                far[p][q] = far[p][q] + in_left[p][q] + in_right[p][q]
                return carry

            lax.fori_loop(0, SLOTS, body, 0)
            for q in range(SLOTS):
                pltpu.make_async_copy(*out_copy(p, q)).start()

    def sum_all(t):
        load(t, 0)
        load(t, 1)
        add_up(t, 0)
        load(t, 2)
        add_up(t, 1)
        add_up(t, 2)

    core0 = me["k"] == 0
    at_root = (me["z"] == 0) & (me["y"] == 0) & (me["x"] == 0) & core0

    def spread_inverse(event, p):
        d, e, f = ORDERS[p]
        start, size, width = BANDS[p]
        part = square.at[pl.ds(start, size), pl.ds(0, width)]
        on = (at_root, (me[e] == 0) & (me[f] == 0) & core0, (me[f] == 0) & core0, core0)

        def sends(n):
            axis = ORDERS[p][n // 2] if n < 6 else "k"
            if n % 2 == 0:
                senders = on[n // 2] if n == 6 else on[n // 2] & (me[axis] == 0)
            else:
                senders = on[n // 2 + 1] & (me[axis] == 1)
            copies = [
                pltpu.make_async_remote_copy(
                    src_ref=part,
                    dst_ref=part,
                    send_sem=send_s.at[p, n, i],
                    recv_sem=recv_s.at[p],
                    device_id=device(moved(me, **{axis: step})),
                    device_id_type=MESH,
                )
                for i, step in enumerate((1, 3) if n in (0, 2, 4) else (1,))
            ]
            return senders, copies

        def receivers(n):
            if n == 6:
                return me["k"] == 1
            axis = ORDERS[p][n // 2]
            mine = on[n // 2 + 1]
            if n % 2 == 0:
                return mine & ((me[axis] == 1) | (me[axis] == 3))
            return mine & (me[axis] == 2)

        if event > 0:

            @pl.when(receivers(event - 1))
            def _():
                pltpu.make_async_copy(part, part, recv_s.at[p]).wait()

            senders, copies = sends(event - 1)

            @pl.when(senders)
            def _():
                for copy in copies:
                    copy.wait_send()

        if event < 7:
            senders, copies = sends(event)

            @pl.when(senders)
            def _():
                for copy in copies:
                    copy.start()

    def factor_steps(low, high):
        @pl.when(at_root)
        def _():
            if low == 0:
                corner = front.at[pl.ds(0, P_SIZE), pl.ds(0, P_SIZE)]
                copy = pltpu.make_async_copy(corner, work, corner_sem.at[0])
                copy.start()
                copy.wait()
            factor_blocks(work, inverse, low, high)
            if high == 4:
                copies = [pltpu.make_async_copy(work, factor_out, corner_sem.at[0])]
                for p in range(3):
                    start, size, width = BANDS[p]
                    copies.append(
                        pltpu.make_async_copy(
                            inverse.at[pl.ds(start, size), pl.ds(0, width)],
                            square.at[pl.ds(start, size), pl.ds(0, width)],
                            corner_sem.at[p + 1],
                        )
                    )
                for copy in copies:
                    copy.start()
                for copy in copies:
                    copy.wait()

    for p in range(3):
        pack(0, p)
    for pool in pools:
        pool[64] = jnp.zeros((max(ROWS), 128), jnp.float32)
    pl.semaphore_wait(barrier, len(partners))
    for p in range(3):
        start_a(0, p)
    factor_steps(0, 2)
    for t in range(4):
        for p in range(3):
            start_b(t, p)
            if t + 1 < 4:
                wait_send_a(t, p)
                pack(t + 1, p)
                start_a(t + 1, p)
        if t == 0:
            factor_steps(2, 4)
        else:
            for p in range(3):
                spread_inverse(2 * t - 1, p)
            sum_all(t - 1)
        for p in range(3):
            spread_inverse(2 * t, p)
    sum_all(3)
    for p in range(3):
        spread_inverse(7, p)
        wait_send_a(3, p)
        for t in range(4):
            part = middle[p].at[t, pl.ds(0, 48)]
            pltpu.make_async_copy(part, part, send_b.at[t, p]).wait()
        whole = far[p]
        pltpu.make_async_copy(whole, whole, out_sem.at[p]).wait()


def exchange(where, prev, last, child_tiles, front_matrix):
    f32 = jnp.float32
    scratch = [pltpu.VMEM((8, 4, 2, r, 128), f32) for r in ROWS]
    scratch += [pltpu.VMEM((65, max(ROWS), 128), f32)] * 2
    for _ in range(6):
        scratch += [pltpu.VMEM((SLOTS, r, 128), f32) for r in ROWS]
    scratch += [pltpu.SemaphoreType.DMA((4, 3))] * 6
    scratch += [pltpu.SemaphoreType.DMA((3,))] * 3
    scratch += [pltpu.SemaphoreType.DMA((3, 7, 2)), pltpu.SemaphoreType.DMA((3,))]
    scratch += [pltpu.SemaphoreType.DMA((4,))]
    scratch += [pltpu.VMEM((P_SIZE, P_SIZE), f32)] * 2
    anywhere = pl.BlockSpec(memory_space=pl.ANY)
    outs = [jax.ShapeDtypeStruct(front_matrix.shape, f32)]
    outs += [jax.ShapeDtypeStruct((4, 4, 16, r, 128), f32) for r in ROWS]
    outs += [jax.ShapeDtypeStruct((4, 64, r, 128), f32) for r in ROWS]
    outs += [jax.ShapeDtypeStruct((P_SIZE, P_SIZE), f32)] * 2
    results = pl.pallas_call(
        exchange_kernel,
        out_shape=outs,
        in_specs=[pl.BlockSpec(memory_space=pltpu.SMEM)] * 3
        + [pl.BlockSpec(memory_space=pltpu.VMEM), anywhere],
        out_specs=[anywhere] * 9,
        scratch_shapes=scratch,
        compiler_params=pltpu.CompilerParams(
            collective_id=1, has_side_effects=True, vmem_limit_bytes=(63 << 20) + (1 << 19)
        ),
        name="exchange",
    )(where, prev, last, child_tiles, front_matrix)
    return results[0], results[7], results[8]


def routing(owner_index, slot_index):
    count = owner_index.shape[0]
    item = lax.broadcasted_iota(jnp.int32, (count, count), 0)
    other = lax.broadcasted_iota(jnp.int32, (count, count), 1)
    same = (owner_index[:, None] == owner_index[None, :]) & (item > other)
    place = owner_index * 2 + jnp.sum(same.astype(jnp.int32), axis=1)
    hit = place[:, None] == lax.broadcasted_iota(jnp.int32, (count, 256), 1)
    where = jnp.sum(jnp.where(hit, lax.broadcasted_iota(jnp.int32, hit.shape, 0), 0), axis=0)
    slots = jnp.sum(jnp.where(hit, slot_index[:, None] + 1, 0), axis=0) - 1
    own = jnp.concatenate([slots.reshape(2, 128), jnp.zeros((6, 128), jnp.int32)], 0)
    table = share_table(own).reshape(128, 8, 128)[:, 0:2].reshape(128, 256).astype(jnp.float32)
    me = position()
    pick_source, pick_owner = [], []
    source = jnp.arange(128)
    source = {"z": source // 32, "k": source // 16 % 2, "y": source // 4 % 4, "x": source % 4}
    place = jnp.arange(256)
    target = {"z": place // 64, "k": place // 32 % 2, "y": place // 8 % 4, "x": place // 2 % 4}
    for p in range(3):
        d, e, f = ORDERS[p]
        r = jnp.arange(32)
        pick_source.append(
            (source[e][None] == (r // 8)[:, None])
            & (source[d][None] == (r // 2 % 4)[:, None])
            & (source["k"][None] == (r % 2)[:, None])
            & (source[f] == me[f])[None]
        )
        n = jnp.arange(8)
        shift = jnp.array(SHIFTS)[n // 2]
        pick_owner.append(
            (target[d] == me[d])[:, None]
            & (target["k"] == me["k"])[:, None]
            & (target[e] == me[e])[:, None]
            & (target[f][:, None] == ((me[f] + shift) % 4)[None])
            & ((place % 2)[:, None] == (n % 2)[None])
        )
    rows = jnp.dot(
        jnp.concatenate(pick_source, 0).astype(jnp.float32),
        table,
        precision=lax.Precision.HIGHEST,
    )
    entries = jnp.stack(
        [
            jnp.dot(rows[p * 32 : p * 32 + 32], pick_owner[p].astype(jnp.float32))
            for p in range(3)
        ]
    )
    entries = entries.reshape(3, 32, 4, 2).transpose(0, 2, 1, 3).reshape(12, 64)
    entries = jnp.round(entries).astype(jnp.int32)
    k = lax.broadcasted_iota(jnp.int32, (12, 64, 64), 1)
    j = lax.broadcasted_iota(jnp.int32, (12, 64, 64), 2)
    match = (entries[:, :, None] == entries[:, None, :]) & (entries[:, :, None] >= 0) & (j < k)
    prev = jnp.max(jnp.where(match, j, -1), axis=2)
    prev = jnp.where(prev < 0, 64, prev)
    q = lax.broadcasted_iota(jnp.int32, (12, SLOTS, 64), 1)
    j = lax.broadcasted_iota(jnp.int32, (12, SLOTS, 64), 2)
    last = jnp.max(jnp.where(entries[:, None, :] == q, j, -1), axis=2)
    last = jnp.where(last < 0, 64, last)
    return where, prev.reshape(-1), last.reshape(-1)


def line(me, axis):
    return [moved(me, **{axis: step}) for step in (1, 3, 2)]


def file(me):
    near = [moved(me, z=step, k=core) for step, core in ((1, 0), (3, 0), (1, 1), (3, 1), (2, 0), (2, 1))]
    return near + [moved(me, k=1)]


def greet(barrier, partners):
    for to in partners:
        pl.semaphore_signal(barrier, inc=1, device_id=device(to), device_id_type=MESH)


def table_kernel(own, table, send, recv):
    me = position()
    barrier = pltpu.get_barrier_semaphore()
    partners = file(me) + line(me, "y") + line(me, "x")
    greet(barrier, partners)
    r = me["z"] * 2 + me["k"]
    table[r, me["y"], me["x"]] = own[...]
    pl.semaphore_wait(barrier, len(partners))

    def run(stage, part, targets):
        copies = [
            pltpu.make_async_remote_copy(
                src_ref=part,
                dst_ref=part,
                send_sem=send.at[stage, i],
                recv_sem=recv.at[stage, i],
                device_id=device(to),
                device_id_type=MESH,
            )
            for i, to in enumerate(targets)
        ]
        for copy in copies:
            copy.start()
        for copy in copies:
            copy.wait()

    run(0, table.at[r, me["y"], me["x"]], file(me))
    run(1, table.at[:, me["y"], me["x"]], line(me, "y"))
    run(2, table.at[:, :, me["x"]], line(me, "x"))


def share_table(own):
    return pl.pallas_call(
        table_kernel,
        out_shape=jax.ShapeDtypeStruct((8, 4, 4, 8, 128), jnp.int32),
        in_specs=[pl.BlockSpec(memory_space=pltpu.VMEM)],
        out_specs=pl.BlockSpec(memory_space=pltpu.VMEM),
        scratch_shapes=[pltpu.SemaphoreType.DMA((3, 7))] * 2,
        compiler_params=pltpu.CompilerParams(collective_id=2, has_side_effects=True),
        name="share_table",
    )(own)


def panel_kernel(assembled, rows, columns, send0, recv0, send1, recv1, send_x, recv_x, send_y, recv_y, send_z, recv_z):
    me = position()
    r = me["z"] * 2 + me["k"]
    y, x = me["y"], me["x"]
    c = y * 4 + x
    depth = rows.shape[2]
    half = depth // 2
    barrier = pltpu.get_barrier_semaphore()
    first = c == 0
    to_row, to_col = lax.rem(c, 8), 2 * r + c // 8
    from_row, from_col = c // 2, r + 8 * lax.rem(c, 2)
    stays = (to_row == r) & (to_col == c)
    partners = file(me) + line(me, "y") + line(me, "x")
    greet(barrier, partners)

    @pl.when(c != 0)
    def _():
        pl.semaphore_signal(barrier, inc=1, device_id=(r, 0), device_id_type=MESH)

    @pl.when(jnp.logical_not(stays))
    def _():
        pl.semaphore_signal(barrier, inc=1, device_id=(from_row, from_col), device_id_type=MESH)

    others = jnp.where(first, 15, 0) + jnp.where(stays, 0, 1)
    pl.semaphore_wait(barrier, len(partners) + others)

    @pl.when(first)
    def _():
        for j in (5, 10, 15, 1, 4, 3, 12, 6, 9, 7, 13, 11, 14, 2, 8):
            pltpu.make_async_remote_copy(
                src_ref=assembled.at[pl.ds(j * depth, depth), pl.ds(0, P_SIZE)],
                dst_ref=rows.at[j // 4, j % 4],
                send_sem=send0,
                recv_sem=recv0,
                device_id=(r, j),
                device_id_type=MESH,
            ).start()
        pltpu.make_async_copy(
            assembled.at[pl.ds(0, depth), pl.ds(0, P_SIZE)], rows.at[0, 0], recv0
        ).start()

    mine = rows.at[y, x]
    pltpu.make_async_copy(mine, mine, recv0).wait()

    low, high = pl.ds(0, half), pl.ds(half, depth - half)

    def spread(part, targets, send, recv):
        copies = [
            pltpu.make_async_remote_copy(
                src_ref=part,
                dst_ref=part,
                send_sem=send.at[i],
                recv_sem=recv.at[i],
                device_id=device(to),
                device_id_type=MESH,
            )
            for i, to in enumerate(targets)
        ]
        for copy in copies:
            copy.start()
        return copies

    def finish(copies):
        for copy in copies:
            copy.wait()

    @pl.when(jnp.logical_not(stays))
    def _():
        pltpu.make_async_remote_copy(
            src_ref=mine,
            dst_ref=columns.at[to_row],
            send_sem=send1,
            recv_sem=recv1,
            device_id=(to_row, to_col),
            device_id_type=MESH,
        ).start()

    @pl.when(stays)
    def _():
        pltpu.make_async_copy(mine, columns.at[r], recv1).start()

    a1 = spread(rows.at[y, x, low], line(me, "x"), send_x.at[0], recv_x.at[0])
    b1 = spread(rows.at[y, x, high], line(me, "y"), send_y.at[0], recv_y.at[0])
    held = columns.at[r]
    pltpu.make_async_copy(held, held, recv1).wait()
    z1 = spread(held, file(me), send_z, recv_z)
    finish(a1)
    a2 = spread(rows.at[y, :, low], line(me, "y"), send_y.at[1], recv_y.at[1])
    finish(b1)
    b2 = spread(rows.at[:, x, high], line(me, "x"), send_x.at[1], recv_x.at[1])
    finish(z1)
    finish(a2)
    finish(b2)

    @pl.when(jnp.logical_not(stays))
    def _():
        pltpu.make_async_copy(mine, mine, send1).wait()

    @pl.when(first)
    def _():
        whole = assembled.at[pl.ds(depth, 15 * depth), pl.ds(0, P_SIZE)]
        pltpu.make_async_copy(whole, whole, send0).wait()


def share_panel(assembled):
    depth = assembled.shape[0] // 16
    anywhere = pl.BlockSpec(memory_space=pl.ANY)
    dma = pltpu.SemaphoreType.DMA
    return pl.pallas_call(
        panel_kernel,
        out_shape=[
            jax.ShapeDtypeStruct((4, 4, depth, P_SIZE), jnp.float32),
            jax.ShapeDtypeStruct((8, depth, P_SIZE), jnp.float32),
        ],
        in_specs=[anywhere],
        out_specs=[anywhere] * 2,
        scratch_shapes=[dma, dma, dma, dma, dma((2, 3)), dma((2, 3)), dma((2, 3)), dma((2, 3)), dma((7,)), dma((7,))],
        compiler_params=pltpu.CompilerParams(collective_id=3, has_side_effects=True),
        name="share_panel",
    )(assembled)


def factor_blocks(work, inverse, first, last):
    n = P_SIZE
    f32 = jnp.float32
    highest = lax.Precision.HIGHEST

    def times(a, b, dims):
        return lax.dot_general(a, b, (dims, ((), ())), precision=highest, preferred_element_type=f32)

    if first == 0:
        block = work[...]
        work[...] = 0.5 * (block + block.T)
        inverse[...] = jnp.zeros((n, n), f32)
    row128 = lax.broadcasted_iota(jnp.int32, (128, 128), 0)
    col128 = lax.broadcasted_iota(jnp.int32, (128, 128), 1)
    row8 = lax.broadcasted_iota(jnp.int32, (8, 1), 0)

    def step(b, carry):
        here = pl.ds(pl.multiple_of(b * 128, 128), 128)
        corner = work[here, here]
        eye = (row128 == col128).astype(f32)
        up = [corner[8 * g : 8 * g + 8] for g in range(16)]
        low = [eye[8 * g : 8 * g + 8] for g in range(16)]
        for j in range(128):
            g, s = j // 8, j % 8
            pivot = up[g][s : s + 1, j : j + 1]
            scale = 1.0 / pivot
            row = up[g][s : s + 1] * scale
            other = low[g][s : s + 1] * scale
            for i in range(g, 16):
                column = up[i][:, j : j + 1]
                if i == g:
                    column = jnp.where(row8 > s, column, 0.0)
                up[i] = up[i] - column * row
                low[i] = low[i] - column * other
        upper = jnp.concatenate(up, 0)
        lower = jnp.concatenate(low, 0)
        pivots = jnp.sum(jnp.where(row128 == col128, upper, 0.0), axis=1, keepdims=True)
        scale = lax.rsqrt(pivots)
        corner_factor = jnp.where(row128 <= col128, upper * scale, 0.0).T
        corner_inverse = jnp.where(row128 >= col128, lower * scale, 0.0)
        below = times(work[:, here], corner_inverse, ((1,), (1,)))
        row = lax.broadcasted_iota(jnp.int32, (n, 128), 0)
        below = jnp.where(row >= b * 128 + 128, below, 0.0)
        work[...] = work[...] - times(below, below, ((1,), (1,)))
        done = lax.broadcasted_iota(jnp.int32, (128, n), 1) < b * 128
        left = times(jnp.where(done, work[here, :], 0.0), inverse[...], ((1,), (0,)))
        inverse[here, :] = -times(corner_inverse, left, ((1,), (0,)))
        inverse[here, here] = corner_inverse
        work[:, here] = below
        work[here, here] = corner_factor
        return carry

    lax.fori_loop(first, last, step, 0)


def split(value):
    high = value.astype(jnp.bfloat16)
    low = (value - high.astype(jnp.float32)).astype(jnp.bfloat16)
    return high, low


def product(a, b):
    def times(x, y):
        return lax.dot_general(x, y, (((1,), (1,)), ((), ())), preferred_element_type=jnp.float32)

    return times(a[0], b[0]) + (times(a[0], b[1]) + times(a[1], b[0]))


def update_kernel(place, rows_raw, columns_raw, inverse, factor, assembled, out, inv_hi, inv_lo, col_hi, col_lo):
    step = pl.program_id(0)
    tile, width = out.shape

    @pl.when(step == 0)
    def _():
        row = lax.broadcasted_iota(jnp.int32, inverse.shape, 0)
        col = lax.broadcasted_iota(jnp.int32, inverse.shape, 1)
        high, low = split(jnp.where(row >= col, inverse[...], 0.0))
        inv_hi[...] = high
        inv_lo[...] = low
        high, low = split(product(split(columns_raw[...]), (high, low)))
        col_hi[...] = high
        col_lo[...] = low

    row_start = place[0] + step * tile
    col_start = place[1]
    panel = product(split(rows_raw[...]), (inv_hi[...], inv_lo[...]))
    change = product(split(panel), (col_hi[...], col_lo[...]))
    row = row_start + lax.broadcasted_iota(jnp.int32, (tile, width), 0)
    col = col_start + lax.broadcasted_iota(jnp.int32, (tile, width), 1)
    out[...] = assembled[...] - jnp.where((row >= col) & (col >= P_SIZE), change, 0.0)

    @pl.when(col_start == 0)
    def _():
        out[:, 0:P_SIZE] = panel

    @pl.when((col_start == 0) & (row_start < P_SIZE))
    def _():
        out[:, 0:P_SIZE] = factor[...]


def update(place, rows_raw, columns_raw, inverse, factor, assembled):
    rows, width = assembled.shape
    tile = 256
    whole = lambda shape: pl.BlockSpec(shape, lambda i: (0, 0))
    bf16 = jnp.bfloat16
    return pl.pallas_call(
        update_kernel,
        grid=(rows // tile,),
        out_shape=jax.ShapeDtypeStruct((rows, width), jnp.float32),
        in_specs=[
            pl.BlockSpec(memory_space=pltpu.SMEM),
            pl.BlockSpec((tile, P_SIZE), lambda i: (i, 0)),
            whole((width, P_SIZE)),
            whole((P_SIZE, P_SIZE)),
            pl.BlockSpec((tile, P_SIZE), lambda i: (jnp.minimum(i, P_SIZE // tile - 1), 0)),
            pl.BlockSpec((tile, width), lambda i: (i, 0)),
        ],
        out_specs=pl.BlockSpec((tile, width), lambda i: (i, 0)),
        scratch_shapes=[
            pltpu.VMEM((P_SIZE, P_SIZE), bf16),
            pltpu.VMEM((P_SIZE, P_SIZE), bf16),
            pltpu.VMEM((width, P_SIZE), bf16),
            pltpu.VMEM((width, P_SIZE), bf16),
        ],
        compiler_params=pltpu.CompilerParams(vmem_limit_bytes=48 << 20),
        name="update",
    )(place, rows_raw, columns_raw, inverse, factor, assembled)


def local(front_matrix, child_tiles, owner_index, slot_index):
    where, prev, last = routing(owner_index, slot_index)
    assembled, inverse, factor = exchange(where, prev, last, child_tiles, front_matrix)
    rows, columns = share_panel(assembled)
    rows_loc, cols_loc = front_matrix.shape
    place = jnp.stack([lax.axis_index("row") * rows_loc, lax.axis_index("col") * cols_loc])
    return update(
        place.astype(jnp.int32),
        rows.reshape(rows_loc, P_SIZE),
        columns.reshape(cols_loc, P_SIZE),
        inverse,
        factor,
        assembled,
    )


def solution(mesh):
    placed = (P("row", "col"), P(("row", "col"), None, None), P(("row", "col")), P(("row", "col")))
    return jax.shard_map(
        local, mesh=mesh, in_specs=placed, out_specs=P("row", "col"), check_vma=False
    )
```

```python
import functools

import jax
import jax.numpy as jnp
from jax import lax
from jax.experimental import pallas as pl
from jax.experimental.pallas import tpu as pltpu
from jax.sharding import PartitionSpec as P

P_SIZE = 512
MESH = pl.DeviceIdType.MESH
ROWS = (88, 88, 80)
STARTS = (0, 88, 176)
HALF = (40, 40, 40)
ORDERS = ("zxy", "xyz", "yzx")
SHIFTS = (2, 1, 3, 0)
SLOTS = 36
BANDS = ((0, 256, 256), (256, 128, 384), (384, 128, 512))


def position():
    row = lax.axis_index("row")
    col = lax.axis_index("col")
    return {"z": row // 2, "k": lax.rem(row, 2), "y": col // 4, "x": lax.rem(col, 4)}


def device(at):
    return (at["z"] * 2 + at["k"], at["y"] * 4 + at["x"])


def moved(at, **steps):
    to = dict(at)
    for name, step in steps.items():
        to[name] = lax.rem(at[name] + step, 2 if name == "k" else 4)
    return to


def exchange_kernel(
    where_ref,
    own_ref,
    child,
    front,
    out,
    arr0,
    arr1,
    arr2,
    mid0,
    mid1,
    mid2,
    square,
    factor_out,
    tables,
    *scratch,
):
    arrived = (arr0, arr1, arr2)
    middle = (mid0, mid1, mid2)
    staging, pools = scratch[0:3], scratch[3:5]
    got = [pools[p % 2].at[:, pl.ds(0, ROWS[p])] for p in range(3)]
    far, right, left = scratch[5:8], scratch[8:11], scratch[11:14]
    in_far, in_left, in_right = scratch[14:17], scratch[17:20], scratch[20:23]
    send_a, recv_a, send_b, recv_b, send_c, recv_c, load_sem, front_sem, out_sem = scratch[23:32]
    send_s, recv_s, corner_sem, work, inverse, *more = scratch[32:]
    send_t, recv_t, near_t, gathered, tab_vector, tab = more
    me = position()

    barrier = pltpu.get_barrier_semaphore()
    partners = [moved(me, k=1)]
    for axis in "zyx":
        for step in (1, 2, 3):
            for core in (0, 1):
                partners.append(moved(me, **{axis: step, "k": core}))
    for to in partners:
        pl.semaphore_signal(barrier, inc=1, device_id=device(to), device_id_type=MESH)

    def pack(t, p):
        d, e, f = ORDERS[p]
        shift = SHIFTS[t]

        def body(i, carry):
            at = {
                d: i // 16,
                "k": lax.rem(i // 8, 2),
                e: lax.rem(i // 2, 4),
                f: lax.rem(me[f] + shift, 4),
            }
            owner = ((at["z"] * 2 + at["k"]) * 4 + at["y"]) * 4 + at["x"]
            index = where_ref[owner * 2 + lax.rem(i, 2)]
            staging[p][i // 8, lax.rem(i // 2, 4), lax.rem(i, 2)] = child[
                index, STARTS[p] : STARTS[p] + ROWS[p], :
            ]
            return carry

        lax.fori_loop(0, 64, body, 0)

    def group(at, d):
        return at[d] * 2 + at["k"]

    def start_a(t, p):
        d = ORDERS[p][0]
        mine = group(me, d)
        for step, core in ((1, 0), (3, 0), (1, 1), (3, 1), (2, 0), (2, 1), (0, 1)):
            to = moved(me, **{d: step, "k": core})
            pltpu.make_async_remote_copy(
                src_ref=staging[p].at[group(to, d)],
                dst_ref=arrived[p].at[t, :, pl.ds(mine * 2, 2)],
                send_sem=send_a.at[t, p],
                recv_sem=recv_a.at[t, p],
                device_id=device(to),
                device_id_type=MESH,
            ).start()
        pltpu.make_async_copy(
            staging[p].at[mine], arrived[p].at[t, :, pl.ds(mine * 2, 2)], recv_a.at[t, p]
        ).start()

    def wait_send_a(t, p):
        part = staging[p].at[pl.ds(0, 7)]
        pltpu.make_async_copy(part, part, send_a.at[t, p]).wait()

    def start_b(t, p):
        e = ORDERS[p][1]
        whole = arrived[p].at[t]
        pltpu.make_async_copy(whole, whole, recv_a.at[t, p]).wait()
        for step in (1, 3, 2):
            to = moved(me, **{e: step})
            pltpu.make_async_remote_copy(
                src_ref=arrived[p].at[t, to[e]],
                dst_ref=middle[p].at[t, pl.ds(me[e] * 16, 16)],
                send_sem=send_b.at[t, p],
                recv_sem=recv_b.at[t, p],
                device_id=device(to),
                device_id_type=MESH,
            ).start()
        pltpu.make_async_copy(
            arrived[p].at[t, me[e]], middle[p].at[t, pl.ds(me[e] * 16, 16)], recv_b.at[t, p]
        ).start()

    def load(t, p):
        whole = middle[p].at[t]
        pltpu.make_async_copy(whole, whole, recv_b.at[t, p]).wait()
        pltpu.make_async_copy(whole, got[p].at[pl.ds(0, 64)], load_sem.at[p]).start()

    def to_neighbour(source, target, p, kind, step):
        f = ORDERS[p][2]
        return pltpu.make_async_remote_copy(
            src_ref=source,
            dst_ref=target,
            send_sem=send_c.at[kind, p],
            recv_sem=recv_c.at[kind, p],
            device_id=device(moved(me, **{f: step})),
            device_id_type=MESH,
        )

    def far_copies(p):
        low, high = pl.ds(0, HALF[p]), pl.ds(HALF[p], ROWS[p] - HALF[p])
        return (
            to_neighbour(far[p].at[:, low], in_far[p].at[:, low], p, 0, 1),
            to_neighbour(far[p].at[:, high], in_far[p].at[:, high], p, 1, 3),
        )

    def front_copy(p, q):
        rows = pl.ds(q // 6 * 256 + STARTS[p], ROWS[p])
        return front.at[rows, pl.ds(q % 6 * 128, 128)], far[p].at[q], front_sem.at[p]

    def out_copy(p, q):
        rows = pl.ds(q // 6 * 256 + STARTS[p], ROWS[p])
        return far[p].at[q], out.at[rows, pl.ds(q % 6 * 128, 128)], out_sem.at[p]

    def add_up(t, p):
        rows = ROWS[p]
        held = got[p]
        pltpu.make_async_copy(
            middle[p].at[t], held.at[pl.ds(0, 64)], load_sem.at[p]
        ).wait()

        def chain(k, carry):
            held[k] = held[k] + held[tab[t, 2 * p, k]]
            return carry

        lax.fori_loop(0, 64, chain, 0)

        def total(q):
            return held[tab[t, 2 * p + 1, q]]

        half = HALF[p]
        shift = SHIFTS[t]
        if shift == 2:

            def body(q, carry):
                far[p][q] = total(q)
                return carry

            lax.fori_loop(0, SLOTS, body, 0)
            for copy in far_copies(p):
                copy.start()
        elif shift == 1:
            far_copies(p)[0].wait_recv()

            def body(q, carry):
                right[p][q] = total(q)
                right[p][q, 0:half] = right[p][q, 0:half] + in_far[p][q, 0:half]
                return carry

            lax.fori_loop(0, SLOTS, body, 0)
            to_neighbour(right[p], in_left[p], p, 2, 1).start()
        elif shift == 3:
            far_copies(p)[1].wait_recv()

            def body(q, carry):
                left[p][q] = total(q)
                left[p][q, half:rows] = left[p][q, half:rows] + in_far[p][q, half:rows]
                return carry

            lax.fori_loop(0, SLOTS, body, 0)
            to_neighbour(left[p], in_right[p], p, 3, 3).start()
            for copy in far_copies(p):
                copy.wait_send()
            for q in range(SLOTS):
                pltpu.make_async_copy(*front_copy(p, q)).start()
        else:
            whole = far[p]
            pltpu.make_async_copy(whole, whole, front_sem.at[p]).wait()

            def own(q, carry):
                far[p][q] = far[p][q] + total(q)
                return carry

            lax.fori_loop(0, SLOTS, own, 0)
            to_neighbour(right[p], in_left[p], p, 2, 1).wait()
            to_neighbour(left[p], in_right[p], p, 3, 3).wait()

            def body(q, carry):
                far[p][q] = far[p][q] + in_left[p][q] + in_right[p][q]
                return carry

            lax.fori_loop(0, SLOTS, body, 0)
            for q in range(SLOTS):
                pltpu.make_async_copy(*out_copy(p, q)).start()

    def sum_all(t):
        load(t, 0)
        load(t, 1)
        add_up(t, 0)
        load(t, 2)
        add_up(t, 1)
        add_up(t, 2)

    core0 = me["k"] == 0
    at_root = (me["z"] == 0) & (me["y"] == 0) & (me["x"] == 0) & core0

    def spread_inverse(event, p):
        d, e, f = ORDERS[p]
        start, size, width = BANDS[p]
        part = square.at[pl.ds(start, size), pl.ds(0, width)]
        on = (at_root, (me[e] == 0) & (me[f] == 0) & core0, (me[f] == 0) & core0, core0)

        def sends(n):
            axis = ORDERS[p][n // 2] if n < 6 else "k"
            if n % 2 == 0:
                senders = on[n // 2] if n == 6 else on[n // 2] & (me[axis] == 0)
            else:
                senders = on[n // 2 + 1] & (me[axis] == 1)
            copies = [
                pltpu.make_async_remote_copy(
                    src_ref=part,
                    dst_ref=part,
                    send_sem=send_s.at[p, n, i],
                    recv_sem=recv_s.at[p],
                    device_id=device(moved(me, **{axis: step})),
                    device_id_type=MESH,
                )
                for i, step in enumerate((1, 3) if n in (0, 2, 4) else (1,))
            ]
            return senders, copies

        def receivers(n):
            if n == 6:
                return me["k"] == 1
            axis = ORDERS[p][n // 2]
            mine = on[n // 2 + 1]
            if n % 2 == 0:
                return mine & ((me[axis] == 1) | (me[axis] == 3))
            return mine & (me[axis] == 2)

        if event > 0:

            @pl.when(receivers(event - 1))
            def _():
                pltpu.make_async_copy(part, part, recv_s.at[p]).wait()

            senders, copies = sends(event - 1)

            @pl.when(senders)
            def _():
                for copy in copies:
                    copy.wait_send()

        if event < 7:
            senders, copies = sends(event)

            @pl.when(senders)
            def _():
                for copy in copies:
                    copy.start()

    def factor_steps(low, high):
        @pl.when(at_root)
        def _():
            if low == 0:
                corner = front.at[pl.ds(0, P_SIZE), pl.ds(0, P_SIZE)]
                copy = pltpu.make_async_copy(corner, work, corner_sem.at[0])
                copy.start()
                copy.wait()
            factor_blocks(work, inverse, low, high)
            if high == 4:
                copies = [pltpu.make_async_copy(work, factor_out, corner_sem.at[0])]
                for p in range(3):
                    start, size, width = BANDS[p]
                    copies.append(
                        pltpu.make_async_copy(
                            inverse.at[pl.ds(start, size), pl.ds(0, width)],
                            square.at[pl.ds(start, size), pl.ds(0, width)],
                            corner_sem.at[p + 1],
                        )
                    )
                for copy in copies:
                    copy.start()
                for copy in copies:
                    copy.wait()

    row_here = me["z"] * 2 + me["k"]

    def table_copies(stage):
        if stage == 0:
            part = tables.at[row_here, me["y"], me["x"]]
            source = own_ref
            targets = [moved(me, z=step, k=core) for step in (1, 3, 2) for core in (0, 1)]
            targets.append(moved(me, k=1))
        elif stage == 1:
            source = part = tables.at[pl.ds(0, 8), me["y"], me["x"]]
            targets = [moved(me, y=step) for step in (1, 3, 2)]
        else:
            source = part = tables.at[pl.ds(0, 8), pl.ds(0, 4), me["x"]]
            targets = [moved(me, x=step) for step in (1, 3, 2)]
        return [
            pltpu.make_async_remote_copy(
                src_ref=source,
                dst_ref=part,
                send_sem=send_t.at[stage, i],
                recv_sem=recv_t.at[stage],
                device_id=device(to),
                device_id_type=MESH,
            )
            for i, to in enumerate(targets)
        ]

    def share_table(stage):
        if stage == 0:
            pltpu.make_async_copy(
                own_ref, tables.at[row_here, me["y"], me["x"]], recv_t.at[0]
            ).start()
        elif stage == 1:
            part = tables.at[pl.ds(0, 8), me["y"], me["x"]]
            pltpu.make_async_copy(part, part, recv_t.at[0]).wait()
        elif stage == 2:
            part = tables.at[pl.ds(0, 8), pl.ds(0, 3), me["x"]]
            pltpu.make_async_copy(part, part, recv_t.at[1]).wait()
        else:
            part = tables.at[pl.ds(0, 8), pl.ds(0, 4), pl.ds(0, 3)]
            pltpu.make_async_copy(part, part, recv_t.at[2]).wait()
        if stage < 3:
            for copy in table_copies(stage):
                copy.start()

    def make_tables():
        for p in range(3):
            d, e, f = ORDERS[p]
            copies = []
            for step in range(4):
                if p == 0:
                    pieces = [(tables.at[pl.ds(0, 8), me["y"], step], step * 8, 8)]
                elif p == 1:
                    pieces = [
                        (tables.at[me["z"] * 2 + k, step, pl.ds(0, 4)], step * 8 + k * 4, 4)
                        for k in range(2)
                    ]
                else:
                    pieces = [
                        (tables.at[step * 2 + k, pl.ds(0, 4), me["x"]], step * 8 + k * 4, 4)
                        for k in range(2)
                    ]
                for source, start, size in pieces:
                    copies.append(
                        pltpu.make_async_copy(
                            source, gathered.at[pl.ds(start, size)], near_t.at[len(copies)]
                        )
                    )
            for copy in copies:
                copy.start()
            for copy in copies:
                copy.wait()
            entry = lax.broadcasted_iota(jnp.int32, (64, 128), 0)
            lane = lax.broadcasted_iota(jnp.int32, (64, 128), 1)
            source = lax.rem(entry, 32)
            if p > 0:
                source = source // 8 * 8 + lax.rem(source, 4) * 2 + lax.rem(source // 4, 2)
            order = source * 2 + entry // 32
            for t in range(4):
                at = dict(me)
                at[f] = lax.rem(me[f] + SHIFTS[t], 4)
                place = (((at["z"] * 2 + at["k"]) * 4 + at["y"]) * 4 + at["x"]) * 2
                sub = lax.broadcasted_iota(jnp.int32, (32, 8, 128), 1)
                picked = jnp.sum(jnp.where(sub == place // 128, gathered[...], 0), axis=1)
                column = lax.rem(place, 128)
                lane32 = lax.broadcasted_iota(jnp.int32, (32, 128), 1)
                slots = jnp.concatenate(
                    [
                        jnp.broadcast_to(
                            jnp.sum(
                                jnp.where(lane32 == column + c, picked, 0), axis=1, keepdims=True
                            ),
                            (32, 128),
                        )
                        for c in range(2)
                    ],
                    0,
                )
                in_row = jnp.sum(jnp.where(order == lane, slots, 0), axis=0, keepdims=True)
                match = (slots == in_row) & (slots >= 0) & (order < lane)
                prev = jnp.max(jnp.where(match, order, -1), axis=0, keepdims=True)
                last = jnp.max(jnp.where(slots == lane, order, -1), axis=0, keepdims=True)
                tab_vector[t, 2 * p : 2 * p + 1, :] = jnp.where(prev < 0, 64, prev)
                tab_vector[t, 2 * p + 1 : 2 * p + 2, :] = jnp.where(last < 0, 64, last)
        copy = pltpu.make_async_copy(tab_vector, tab, near_t.at[0])
        copy.start()
        copy.wait()
        for stage in range(3):
            for copy in table_copies(stage):
                copy.wait_send()

    for p in range(3):
        pack(0, p)
    for pool in pools:
        pool[64] = jnp.zeros((max(ROWS), 128), jnp.float32)
    pl.semaphore_wait(barrier, len(partners))
    share_table(0)
    for p in range(3):
        start_a(0, p)
    share_table(1)
    factor_steps(0, 2)
    for t in range(4):
        for p in range(3):
            start_b(t, p)
            if t + 1 < 4:
                wait_send_a(t, p)
                pack(t + 1, p)
                start_a(t + 1, p)
        if t == 0:
            share_table(2)
            factor_steps(2, 4)
        else:
            for p in range(3):
                spread_inverse(2 * t - 1, p)
            if t == 1:
                share_table(3)
                make_tables()
            sum_all(t - 1)
        for p in range(3):
            spread_inverse(2 * t, p)
    sum_all(3)
    for p in range(3):
        spread_inverse(7, p)
        wait_send_a(3, p)
        for t in range(4):
            part = middle[p].at[t, pl.ds(0, 48)]
            pltpu.make_async_copy(part, part, send_b.at[t, p]).wait()
        whole = far[p]
        pltpu.make_async_copy(whole, whole, out_sem.at[p]).wait()


def exchange(where, own, child_tiles, front_matrix):
    f32 = jnp.float32
    scratch = [pltpu.VMEM((8, 4, 2, r, 128), f32) for r in ROWS]
    scratch += [pltpu.VMEM((65, max(ROWS), 128), f32)] * 2
    for _ in range(6):
        scratch += [pltpu.VMEM((SLOTS, r, 128), f32) for r in ROWS]
    scratch += [pltpu.SemaphoreType.DMA((4, 3))] * 6
    scratch += [pltpu.SemaphoreType.DMA((3,))] * 3
    scratch += [pltpu.SemaphoreType.DMA((3, 7, 2)), pltpu.SemaphoreType.DMA((3,))]
    scratch += [pltpu.SemaphoreType.DMA((4,))]
    scratch += [pltpu.VMEM((P_SIZE, P_SIZE), f32)] * 2
    scratch += [pltpu.SemaphoreType.DMA((3, 7)), pltpu.SemaphoreType.DMA((3,))]
    scratch += [pltpu.SemaphoreType.DMA((8,)), pltpu.VMEM((32, 8, 128), jnp.int32)]
    scratch += [pltpu.VMEM((4, 8, 128), jnp.int32), pltpu.SMEM((4, 8, 128), jnp.int32)]
    anywhere = pl.BlockSpec(memory_space=pl.ANY)
    outs = [jax.ShapeDtypeStruct(front_matrix.shape, f32)]
    outs += [jax.ShapeDtypeStruct((4, 4, 16, r, 128), f32) for r in ROWS]
    outs += [jax.ShapeDtypeStruct((4, 64, r, 128), f32) for r in ROWS]
    outs += [jax.ShapeDtypeStruct((P_SIZE, P_SIZE), f32)] * 2
    outs += [jax.ShapeDtypeStruct((8, 4, 4, 8, 128), jnp.int32)]
    results = pl.pallas_call(
        exchange_kernel,
        out_shape=outs,
        in_specs=[pl.BlockSpec(memory_space=pltpu.SMEM)]
        + [pl.BlockSpec(memory_space=pltpu.VMEM)] * 2
        + [anywhere],
        out_specs=[anywhere] * 10,
        scratch_shapes=scratch,
        compiler_params=pltpu.CompilerParams(
            collective_id=1, has_side_effects=True, vmem_limit_bytes=(63 << 20) + (1 << 19)
        ),
        name="exchange",
    )(where, own, child_tiles, front_matrix)
    return results[0], results[7], results[8]


def routing(owner_index, slot_index):
    count = owner_index.shape[0]
    item = lax.broadcasted_iota(jnp.int32, (count, count), 0)
    other = lax.broadcasted_iota(jnp.int32, (count, count), 1)
    same = (owner_index[:, None] == owner_index[None, :]) & (item > other)
    place = owner_index * 2 + jnp.sum(same.astype(jnp.int32), axis=1)
    hit = place[:, None] == lax.broadcasted_iota(jnp.int32, (count, 256), 1)
    where = jnp.sum(jnp.where(hit, lax.broadcasted_iota(jnp.int32, hit.shape, 0), 0), axis=0)
    slots = jnp.sum(jnp.where(hit, slot_index[:, None] + 1, 0), axis=0) - 1
    own = jnp.concatenate([slots.reshape(2, 128), jnp.zeros((6, 128), jnp.int32)], 0)
    return where, own


def line(me, axis):
    return [moved(me, **{axis: step}) for step in (1, 3, 2)]


def file(me):
    near = [moved(me, z=step, k=core) for step, core in ((1, 0), (3, 0), (1, 1), (3, 1), (2, 0), (2, 1))]
    return near + [moved(me, k=1)]


def greet(barrier, partners):
    for to in partners:
        pl.semaphore_signal(barrier, inc=1, device_id=device(to), device_id_type=MESH)


def panel_kernel(
    assembled, rows, columns, low_stage, high_stage, send0, recv0, send1, recv1, send2, recv2, send_x, recv_x, send_y, recv_y, send_z, recv_z
):
    me = position()
    r = me["z"] * 2 + me["k"]
    y, x = me["y"], me["x"]
    c = y * 4 + x
    depth = rows.shape[2]
    half = depth // 2
    low, high = pl.ds(0, half), pl.ds(half, depth - half)
    wide = pl.ds(0, P_SIZE)
    barrier = pltpu.get_barrier_semaphore()
    to_row, to_col = lax.rem(c, 8), 2 * r + c // 8
    from_row, from_col = c // 2, r + 8 * lax.rem(c, 2)
    stays = (to_row == r) & (to_col == c)
    partners = file(me) + line(me, "y") + line(me, "x")
    greet(barrier, partners)

    @pl.when(jnp.logical_not(stays))
    def _():
        pl.semaphore_signal(barrier, inc=1, device_id=(from_row, from_col), device_id_type=MESH)

    pl.semaphore_wait(barrier, len(partners) + jnp.where(stays, 0, 1))

    def remote(source, target, send, recv, to):
        return pltpu.make_async_remote_copy(
            src_ref=source,
            dst_ref=target,
            send_sem=send,
            recv_sem=recv,
            device_id=to,
            device_id_type=MESH,
        )

    steps = (1, 3, 2)

    def root_copies():
        copies = []
        for i, step in enumerate(steps):
            copies.append(
                remote(
                    assembled.at[:, step, low, wide],
                    low_stage,
                    send0.at[0, i],
                    recv0.at[0],
                    device(moved(me, x=step)),
                )
            )
            copies.append(
                remote(
                    assembled.at[step, :, high, wide],
                    high_stage,
                    send0.at[1, i],
                    recv0.at[1],
                    device(moved(me, y=step)),
                )
            )
        return copies

    def low_copies():
        return [
            remote(
                low_stage.at[step],
                rows.at[step, x, low],
                send1.at[0, i],
                recv1.at[0],
                device(moved(me, y=step)),
            )
            for i, step in enumerate(steps)
        ]

    def high_copies():
        return [
            remote(
                high_stage.at[step],
                rows.at[y, step, high],
                send1.at[1, i],
                recv1.at[1],
                device(moved(me, x=step)),
            )
            for i, step in enumerate(steps)
        ]

    at_top, at_side = y == 0, x == 0

    @pl.when(at_top & at_side)
    def _():
        for copy in root_copies():
            copy.start()
        pltpu.make_async_copy(assembled.at[:, 0, low, wide], low_stage, recv0.at[0]).start()
        pltpu.make_async_copy(assembled.at[0, :, high, wide], high_stage, recv0.at[1]).start()

    @pl.when(at_top)
    def _():
        pltpu.make_async_copy(low_stage, low_stage, recv0.at[0]).wait()
        for copy in low_copies():
            copy.start()
        pltpu.make_async_copy(low_stage.at[0], rows.at[0, x, low], recv1.at[0]).start()

    @pl.when(at_side)
    def _():
        pltpu.make_async_copy(high_stage, high_stage, recv0.at[1]).wait()
        for copy in high_copies():
            copy.start()
        pltpu.make_async_copy(high_stage.at[0], rows.at[y, 0, high], recv1.at[1]).start()

    def spread(part, targets, send, recv):
        copies = [
            remote(part, part, send.at[i], recv.at[i], device(to)) for i, to in enumerate(targets)
        ]
        for copy in copies:
            copy.start()
        return copies

    def finish(copies):
        for copy in copies:
            copy.wait()

    mine_low, mine_high = rows.at[y, x, low], rows.at[y, x, high]
    pltpu.make_async_copy(mine_low, mine_low, recv1.at[0]).wait()
    a1 = spread(mine_low, line(me, "x"), send_x.at[0], recv_x.at[0])
    pltpu.make_async_copy(mine_high, mine_high, recv1.at[1]).wait()
    b1 = spread(mine_high, line(me, "y"), send_y.at[0], recv_y.at[0])
    mine = rows.at[y, x]

    @pl.when(jnp.logical_not(stays))
    def _():
        remote(mine, columns.at[to_row], send2, recv2, (to_row, to_col)).start()

    @pl.when(stays)
    def _():
        pltpu.make_async_copy(mine, columns.at[r], recv2).start()

    finish(a1)
    a2 = spread(rows.at[y, :, low], line(me, "y"), send_y.at[1], recv_y.at[1])
    finish(b1)
    b2 = spread(rows.at[:, x, high], line(me, "x"), send_x.at[1], recv_x.at[1])
    held = columns.at[r]
    pltpu.make_async_copy(held, held, recv2).wait()
    z1 = spread(held, file(me), send_z, recv_z)
    finish(z1)
    finish(a2)
    finish(b2)

    @pl.when(jnp.logical_not(stays))
    def _():
        pltpu.make_async_copy(mine, mine, send2).wait()

    @pl.when(at_top & at_side)
    def _():
        for copy in root_copies():
            copy.wait_send()

    @pl.when(at_top)
    def _():
        for copy in low_copies():
            copy.wait_send()

    @pl.when(at_side)
    def _():
        for copy in high_copies():
            copy.wait_send()


def share_panel(assembled):
    depth = assembled.shape[0] // 16
    half = depth // 2
    anywhere = pl.BlockSpec(memory_space=pl.ANY)
    dma = pltpu.SemaphoreType.DMA
    shapes = ((4, 4, depth, P_SIZE), (8, depth, P_SIZE), (4, half, P_SIZE), (4, depth - half, P_SIZE))
    return pl.pallas_call(
        panel_kernel,
        out_shape=[jax.ShapeDtypeStruct(shape, jnp.float32) for shape in shapes],
        in_specs=[anywhere],
        out_specs=[anywhere] * 4,
        scratch_shapes=[
            dma((2, 3)),
            dma((2,)),
            dma((2, 3)),
            dma((2,)),
            dma,
            dma,
            dma((2, 3)),
            dma((2, 3)),
            dma((2, 3)),
            dma((2, 3)),
            dma((7,)),
            dma((7,)),
        ],
        compiler_params=pltpu.CompilerParams(collective_id=3, has_side_effects=True),
        name="share_panel",
    )(assembled.reshape(4, 4, depth, assembled.shape[1]))[:2]


def factor_blocks(work, inverse, first, last):
    n = P_SIZE
    f32 = jnp.float32
    highest = lax.Precision.HIGHEST

    def times(a, b, dims):
        return lax.dot_general(a, b, (dims, ((), ())), precision=highest, preferred_element_type=f32)

    if first == 0:
        block = work[...]
        work[...] = 0.5 * (block + block.T)
        inverse[...] = jnp.zeros((n, n), f32)
    row128 = lax.broadcasted_iota(jnp.int32, (128, 128), 0)
    col128 = lax.broadcasted_iota(jnp.int32, (128, 128), 1)
    row8 = lax.broadcasted_iota(jnp.int32, (8, 1), 0)

    def step(b, carry):
        here = pl.ds(pl.multiple_of(b * 128, 128), 128)
        corner = work[here, here]
        eye = (row128 == col128).astype(f32)
        up = [corner[8 * g : 8 * g + 8] for g in range(16)]
        low = [eye[8 * g : 8 * g + 8] for g in range(16)]
        for j in range(128):
            g, s = j // 8, j % 8
            pivot = up[g][s : s + 1, j : j + 1]
            scale = 1.0 / pivot
            row = up[g][s : s + 1] * scale
            other = low[g][s : s + 1] * scale
            for i in range(g, 16):
                column = up[i][:, j : j + 1]
                if i == g:
                    column = jnp.where(row8 > s, column, 0.0)
                up[i] = up[i] - column * row
                low[i] = low[i] - column * other
        upper = jnp.concatenate(up, 0)
        lower = jnp.concatenate(low, 0)
        pivots = jnp.sum(jnp.where(row128 == col128, upper, 0.0), axis=1, keepdims=True)
        scale = lax.rsqrt(pivots)
        corner_factor = jnp.where(row128 <= col128, upper * scale, 0.0).T
        corner_inverse = jnp.where(row128 >= col128, lower * scale, 0.0)
        below = times(work[:, here], corner_inverse, ((1,), (1,)))
        row = lax.broadcasted_iota(jnp.int32, (n, 128), 0)
        below = jnp.where(row >= b * 128 + 128, below, 0.0)
        work[...] = work[...] - times(below, below, ((1,), (1,)))
        done = lax.broadcasted_iota(jnp.int32, (128, n), 1) < b * 128
        left = times(jnp.where(done, work[here, :], 0.0), inverse[...], ((1,), (0,)))
        inverse[here, :] = -times(corner_inverse, left, ((1,), (0,)))
        inverse[here, here] = corner_inverse
        work[:, here] = below
        work[here, here] = corner_factor
        return carry

    lax.fori_loop(first, last, step, 0)


def split(value):
    high = value.astype(jnp.bfloat16)
    low = (value - high.astype(jnp.float32)).astype(jnp.bfloat16)
    return high, low


def product(a, b):
    def times(x, y):
        return lax.dot_general(x, y, (((1,), (1,)), ((), ())), preferred_element_type=jnp.float32)

    return times(a[0], b[0]) + (times(a[0], b[1]) + times(a[1], b[0]))


def update_kernel(place, rows_raw, columns_raw, inverse, factor, assembled, out, inv_hi, inv_lo, col_hi, col_lo):
    step = pl.program_id(0)
    tile, width = out.shape

    @pl.when(step == 0)
    def _():
        row = lax.broadcasted_iota(jnp.int32, inverse.shape, 0)
        col = lax.broadcasted_iota(jnp.int32, inverse.shape, 1)
        high, low = split(jnp.where(row >= col, inverse[...], 0.0))
        inv_hi[...] = high
        inv_lo[...] = low
        high, low = split(product(split(columns_raw[...]), (high, low)))
        col_hi[...] = high
        col_lo[...] = low

    row_start = place[0] + step * tile
    col_start = place[1]
    panel = product(split(rows_raw[...]), (inv_hi[...], inv_lo[...]))
    change = product(split(panel), (col_hi[...], col_lo[...]))
    row = row_start + lax.broadcasted_iota(jnp.int32, (tile, width), 0)
    col = col_start + lax.broadcasted_iota(jnp.int32, (tile, width), 1)
    out[...] = assembled[...] - jnp.where((row >= col) & (col >= P_SIZE), change, 0.0)

    @pl.when(col_start == 0)
    def _():
        out[:, 0:P_SIZE] = panel

    @pl.when((col_start == 0) & (row_start < P_SIZE))
    def _():
        out[:, 0:P_SIZE] = factor[...]


def update(place, rows_raw, columns_raw, inverse, factor, assembled):
    rows, width = assembled.shape
    tile = 256
    whole = lambda shape: pl.BlockSpec(shape, lambda i: (0, 0))
    bf16 = jnp.bfloat16
    return pl.pallas_call(
        update_kernel,
        grid=(rows // tile,),
        out_shape=jax.ShapeDtypeStruct((rows, width), jnp.float32),
        in_specs=[
            pl.BlockSpec(memory_space=pltpu.SMEM),
            pl.BlockSpec((tile, P_SIZE), lambda i: (i, 0)),
            whole((width, P_SIZE)),
            whole((P_SIZE, P_SIZE)),
            pl.BlockSpec((tile, P_SIZE), lambda i: (jnp.minimum(i, P_SIZE // tile - 1), 0)),
            pl.BlockSpec((tile, width), lambda i: (i, 0)),
        ],
        out_specs=pl.BlockSpec((tile, width), lambda i: (i, 0)),
        scratch_shapes=[
            pltpu.VMEM((P_SIZE, P_SIZE), bf16),
            pltpu.VMEM((P_SIZE, P_SIZE), bf16),
            pltpu.VMEM((width, P_SIZE), bf16),
            pltpu.VMEM((width, P_SIZE), bf16),
        ],
        compiler_params=pltpu.CompilerParams(vmem_limit_bytes=62 << 20),
        name="update",
    )(place, rows_raw, columns_raw, inverse, factor, assembled)


def local(front_matrix, child_tiles, owner_index, slot_index):
    where, own = routing(owner_index, slot_index)
    assembled, inverse, factor = exchange(where, own, child_tiles, front_matrix)
    rows, columns = share_panel(assembled)
    rows_loc, cols_loc = front_matrix.shape
    place = jnp.stack([lax.axis_index("row") * rows_loc, lax.axis_index("col") * cols_loc])
    return update(
        place.astype(jnp.int32),
        rows.reshape(rows_loc, P_SIZE),
        columns.reshape(cols_loc, P_SIZE),
        inverse,
        factor,
        assembled,
    )


def solution(mesh):
    placed = (P("row", "col"), P(("row", "col"), None, None), P(("row", "col")), P(("row", "col")))
    return jax.shard_map(
        local, mesh=mesh, in_specs=placed, out_specs=P("row", "col"), check_vma=False
    )
```

```python
import functools

import jax
import jax.numpy as jnp
from jax import lax
from jax.experimental import pallas as pl
from jax.experimental.pallas import tpu as pltpu
from jax.sharding import PartitionSpec as P

P_SIZE = 512
MESH = pl.DeviceIdType.MESH
ROWS = (88, 80, 88)
STARTS = (0, 88, 168)
HALF = (40, 40, 40)
ORDERS = ("zxy", "xyz", "yzx")
SHIFTS = (2, 1, 3, 0)
SLOTS = 36
BANDS = ((0, 256, 256), (256, 128, 384), (384, 128, 512))


def position():
    row = lax.axis_index("row")
    col = lax.axis_index("col")
    return {"z": row // 2, "k": lax.rem(row, 2), "y": col // 4, "x": lax.rem(col, 4)}


def device(at):
    return (at["z"] * 2 + at["k"], at["y"] * 4 + at["x"])


def moved(at, **steps):
    to = dict(at)
    for name, step in steps.items():
        to[name] = lax.rem(at[name] + step, 2 if name == "k" else 4)
    return to


def exchange_kernel(
    where_ref,
    own_ref,
    child,
    front,
    out,
    arr0,
    arr1,
    arr2,
    mid0,
    mid1,
    mid2,
    square,
    factor_out,
    tables,
    *scratch,
):
    arrived = (arr0, arr1, arr2)
    middle = (mid0, mid1, mid2)
    staging, pools = scratch[0:3], scratch[3:5]
    got = [pools[p % 2].at[:, pl.ds(0, ROWS[p])] for p in range(3)]
    far, right, left = scratch[5:8], scratch[8:11], scratch[11:14]
    in_far, in_left, in_right = scratch[14:17], scratch[17:20], scratch[20:23]
    send_a, recv_a, send_b, recv_b, send_c, recv_c, load_sem, front_sem, out_sem = scratch[23:32]
    send_s, recv_s, corner_sem, work, inverse, *more = scratch[32:]
    send_t, recv_t, near_t, gathered, tab_vector, tab = more
    me = position()

    barrier = pltpu.get_barrier_semaphore()
    partners = [moved(me, k=1)]
    for axis in "zyx":
        for step in (1, 2, 3):
            for core in (0, 1):
                partners.append(moved(me, **{axis: step, "k": core}))
    for to in partners:
        pl.semaphore_signal(barrier, inc=1, device_id=device(to), device_id_type=MESH)

    def pack(t, p):
        d, e, f = ORDERS[p]
        shift = SHIFTS[t]

        def body(i, carry):
            at = {
                d: i // 16,
                "k": lax.rem(i // 8, 2),
                e: lax.rem(i // 2, 4),
                f: lax.rem(me[f] + shift, 4),
            }
            owner = ((at["z"] * 2 + at["k"]) * 4 + at["y"]) * 4 + at["x"]
            index = where_ref[owner * 2 + lax.rem(i, 2)]
            staging[p][i // 8, lax.rem(i // 2, 4), lax.rem(i, 2)] = child[
                index, STARTS[p] : STARTS[p] + ROWS[p], :
            ]
            return carry

        lax.fori_loop(0, 64, body, 0)

    def group(at, d):
        return at[d] * 2 + at["k"]

    def start_a(t, p):
        d = ORDERS[p][0]
        mine = group(me, d)
        for step, core in ((1, 0), (3, 0), (1, 1), (3, 1), (2, 0), (2, 1), (0, 1)):
            to = moved(me, **{d: step, "k": core})
            pltpu.make_async_remote_copy(
                src_ref=staging[p].at[group(to, d)],
                dst_ref=arrived[p].at[t, :, pl.ds(mine * 2, 2)],
                send_sem=send_a.at[t, p],
                recv_sem=recv_a.at[t, p],
                device_id=device(to),
                device_id_type=MESH,
            ).start()
        pltpu.make_async_copy(
            staging[p].at[mine], arrived[p].at[t, :, pl.ds(mine * 2, 2)], recv_a.at[t, p]
        ).start()

    def wait_send_a(t, p):
        part = staging[p].at[pl.ds(0, 7)]
        pltpu.make_async_copy(part, part, send_a.at[t, p]).wait()

    def start_b(t, p):
        e = ORDERS[p][1]
        whole = arrived[p].at[t]
        pltpu.make_async_copy(whole, whole, recv_a.at[t, p]).wait()
        for step in (1, 3, 2):
            to = moved(me, **{e: step})
            pltpu.make_async_remote_copy(
                src_ref=arrived[p].at[t, to[e]],
                dst_ref=middle[p].at[t, pl.ds(me[e] * 16, 16)],
                send_sem=send_b.at[t, p],
                recv_sem=recv_b.at[t, p],
                device_id=device(to),
                device_id_type=MESH,
            ).start()
        pltpu.make_async_copy(
            arrived[p].at[t, me[e]], middle[p].at[t, pl.ds(me[e] * 16, 16)], recv_b.at[t, p]
        ).start()

    def load(t, p):
        whole = middle[p].at[t]
        pltpu.make_async_copy(whole, whole, recv_b.at[t, p]).wait()
        pltpu.make_async_copy(whole, got[p].at[pl.ds(0, 64)], load_sem.at[p]).start()

    def to_neighbour(source, target, p, kind, step):
        f = ORDERS[p][2]
        return pltpu.make_async_remote_copy(
            src_ref=source,
            dst_ref=target,
            send_sem=send_c.at[kind, p],
            recv_sem=recv_c.at[kind, p],
            device_id=device(moved(me, **{f: step})),
            device_id_type=MESH,
        )

    def far_copies(p):
        low, high = pl.ds(0, HALF[p]), pl.ds(HALF[p], ROWS[p] - HALF[p])
        return (
            to_neighbour(far[p].at[:, low], in_far[p].at[:, low], p, 0, 1),
            to_neighbour(far[p].at[:, high], in_far[p].at[:, high], p, 1, 3),
        )

    def front_copy(p, q):
        rows = pl.ds(q // 6 * 256 + STARTS[p], ROWS[p])
        return front.at[rows, pl.ds(q % 6 * 128, 128)], far[p].at[q], front_sem.at[p]

    def out_copy(p, q):
        rows = pl.ds(q // 6 * 256 + STARTS[p], ROWS[p])
        return far[p].at[q], out.at[rows, pl.ds(q % 6 * 128, 128)], out_sem.at[p]

    def add_up(t, p):
        rows = ROWS[p]
        held = got[p]
        pltpu.make_async_copy(
            middle[p].at[t], held.at[pl.ds(0, 64)], load_sem.at[p]
        ).wait()

        def chain(k, carry):
            held[k] = held[k] + held[tab[t, 2 * p, k]]
            return carry

        lax.fori_loop(0, 64, chain, 0)

        def total(q):
            return held[tab[t, 2 * p + 1, q]]

        half = HALF[p]
        shift = SHIFTS[t]
        if shift == 2:

            def body(q, carry):
                far[p][q] = total(q)
                return carry

            lax.fori_loop(0, SLOTS, body, 0)
            for copy in far_copies(p):
                copy.start()
        elif shift == 1:
            far_copies(p)[0].wait_recv()

            def body(q, carry):
                right[p][q] = total(q)
                right[p][q, 0:half] = right[p][q, 0:half] + in_far[p][q, 0:half]
                return carry

            lax.fori_loop(0, SLOTS, body, 0)
            to_neighbour(right[p], in_left[p], p, 2, 1).start()
        elif shift == 3:
            far_copies(p)[1].wait_recv()

            def body(q, carry):
                left[p][q] = total(q)
                left[p][q, half:rows] = left[p][q, half:rows] + in_far[p][q, half:rows]
                return carry

            lax.fori_loop(0, SLOTS, body, 0)
            to_neighbour(left[p], in_right[p], p, 3, 3).start()
            for copy in far_copies(p):
                copy.wait_send()
            for q in range(SLOTS):
                pltpu.make_async_copy(*front_copy(p, q)).start()
        else:
            whole = far[p]
            pltpu.make_async_copy(whole, whole, front_sem.at[p]).wait()

            def own(q, carry):
                far[p][q] = far[p][q] + total(q)
                return carry

            lax.fori_loop(0, SLOTS, own, 0)
            to_neighbour(right[p], in_left[p], p, 2, 1).wait()
            to_neighbour(left[p], in_right[p], p, 3, 3).wait()

            def body(q, carry):
                far[p][q] = far[p][q] + in_left[p][q] + in_right[p][q]
                return carry

            lax.fori_loop(0, SLOTS, body, 0)
            for q in range(SLOTS):
                pltpu.make_async_copy(*out_copy(p, q)).start()

    def sum_all(t):
        load(t, 0)
        load(t, 1)
        add_up(t, 0)
        load(t, 2)
        add_up(t, 1)
        add_up(t, 2)

    core0 = me["k"] == 0
    at_root = (me["z"] == 0) & (me["y"] == 0) & (me["x"] == 0) & core0

    def spread_inverse(event, p):
        d, e, f = ORDERS[p]
        start, size, width = BANDS[p]
        part = square.at[pl.ds(start, size), pl.ds(0, width)]
        on = (at_root, (me[e] == 0) & (me[f] == 0) & core0, (me[f] == 0) & core0, core0)

        def sends(n):
            axis = ORDERS[p][n // 2] if n < 6 else "k"
            if n % 2 == 0:
                senders = on[n // 2] if n == 6 else on[n // 2] & (me[axis] == 0)
            else:
                senders = on[n // 2 + 1] & (me[axis] == 1)
            copies = [
                pltpu.make_async_remote_copy(
                    src_ref=part,
                    dst_ref=part,
                    send_sem=send_s.at[p, n, i],
                    recv_sem=recv_s.at[p],
                    device_id=device(moved(me, **{axis: step})),
                    device_id_type=MESH,
                )
                for i, step in enumerate((1, 3) if n in (0, 2, 4) else (1,))
            ]
            return senders, copies

        def receivers(n):
            if n == 6:
                return me["k"] == 1
            axis = ORDERS[p][n // 2]
            mine = on[n // 2 + 1]
            if n % 2 == 0:
                return mine & ((me[axis] == 1) | (me[axis] == 3))
            return mine & (me[axis] == 2)

        if event > 0:

            @pl.when(receivers(event - 1))
            def _():
                pltpu.make_async_copy(part, part, recv_s.at[p]).wait()

            senders, copies = sends(event - 1)

            @pl.when(senders)
            def _():
                for copy in copies:
                    copy.wait_send()

        if event < 7:
            senders, copies = sends(event)

            @pl.when(senders)
            def _():
                for copy in copies:
                    copy.start()

    def factor_steps(low, high):
        @pl.when(at_root)
        def _():
            if low == 0:
                corner = front.at[pl.ds(0, P_SIZE), pl.ds(0, P_SIZE)]
                copy = pltpu.make_async_copy(corner, work, corner_sem.at[0])
                copy.start()
                copy.wait()
            factor_blocks(work, inverse, low, high)
            if high == 4:
                copies = [pltpu.make_async_copy(work, factor_out, corner_sem.at[0])]
                for p in range(3):
                    start, size, width = BANDS[p]
                    copies.append(
                        pltpu.make_async_copy(
                            inverse.at[pl.ds(start, size), pl.ds(0, width)],
                            square.at[pl.ds(start, size), pl.ds(0, width)],
                            corner_sem.at[p + 1],
                        )
                    )
                for copy in copies:
                    copy.start()
                for copy in copies:
                    copy.wait()

    row_here = me["z"] * 2 + me["k"]

    def table_copies(stage):
        if stage == 0:
            part = tables.at[row_here, me["y"], me["x"]]
            source = own_ref
            targets = [moved(me, z=step, k=core) for step in (1, 3, 2) for core in (0, 1)]
            targets.append(moved(me, k=1))
        elif stage == 1:
            source = part = tables.at[pl.ds(0, 8), me["y"], me["x"]]
            targets = [moved(me, y=step) for step in (1, 3, 2)]
        else:
            source = part = tables.at[pl.ds(0, 8), pl.ds(0, 4), me["x"]]
            targets = [moved(me, x=step) for step in (1, 3, 2)]
        return [
            pltpu.make_async_remote_copy(
                src_ref=source,
                dst_ref=part,
                send_sem=send_t.at[stage, i],
                recv_sem=recv_t.at[stage],
                device_id=device(to),
                device_id_type=MESH,
            )
            for i, to in enumerate(targets)
        ]

    def share_table(stage):
        if stage == 0:
            pltpu.make_async_copy(
                own_ref, tables.at[row_here, me["y"], me["x"]], recv_t.at[0]
            ).start()
        elif stage == 1:
            part = tables.at[pl.ds(0, 8), me["y"], me["x"]]
            pltpu.make_async_copy(part, part, recv_t.at[0]).wait()
        elif stage == 2:
            part = tables.at[pl.ds(0, 8), pl.ds(0, 3), me["x"]]
            pltpu.make_async_copy(part, part, recv_t.at[1]).wait()
        else:
            part = tables.at[pl.ds(0, 8), pl.ds(0, 4), pl.ds(0, 3)]
            pltpu.make_async_copy(part, part, recv_t.at[2]).wait()
        if stage < 3:
            for copy in table_copies(stage):
                copy.start()

    def make_tables():
        for p in range(3):
            d, e, f = ORDERS[p]
            copies = []
            for step in range(4):
                if p == 0:
                    pieces = [(tables.at[pl.ds(0, 8), me["y"], step], step * 8, 8)]
                elif p == 1:
                    pieces = [
                        (tables.at[me["z"] * 2 + k, step, pl.ds(0, 4)], step * 8 + k * 4, 4)
                        for k in range(2)
                    ]
                else:
                    pieces = [
                        (tables.at[step * 2 + k, pl.ds(0, 4), me["x"]], step * 8 + k * 4, 4)
                        for k in range(2)
                    ]
                for source, start, size in pieces:
                    copies.append(
                        pltpu.make_async_copy(
                            source, gathered.at[pl.ds(start, size)], near_t.at[len(copies)]
                        )
                    )
            for copy in copies:
                copy.start()
            for copy in copies:
                copy.wait()
            entry = lax.broadcasted_iota(jnp.int32, (64, 128), 0)
            lane = lax.broadcasted_iota(jnp.int32, (64, 128), 1)
            source = lax.rem(entry, 32)
            if p > 0:
                source = source // 8 * 8 + lax.rem(source, 4) * 2 + lax.rem(source // 4, 2)
            order = source * 2 + entry // 32
            for t in range(4):
                at = dict(me)
                at[f] = lax.rem(me[f] + SHIFTS[t], 4)
                place = (((at["z"] * 2 + at["k"]) * 4 + at["y"]) * 4 + at["x"]) * 2
                sub = lax.broadcasted_iota(jnp.int32, (32, 8, 128), 1)
                picked = jnp.sum(jnp.where(sub == place // 128, gathered[...], 0), axis=1)
                column = lax.rem(place, 128)
                lane32 = lax.broadcasted_iota(jnp.int32, (32, 128), 1)
                slots = jnp.concatenate(
                    [
                        jnp.broadcast_to(
                            jnp.sum(
                                jnp.where(lane32 == column + c, picked, 0), axis=1, keepdims=True
                            ),
                            (32, 128),
                        )
                        for c in range(2)
                    ],
                    0,
                )
                in_row = jnp.sum(jnp.where(order == lane, slots, 0), axis=0, keepdims=True)
                match = (slots == in_row) & (slots >= 0) & (order < lane)
                prev = jnp.max(jnp.where(match, order, -1), axis=0, keepdims=True)
                last = jnp.max(jnp.where(slots == lane, order, -1), axis=0, keepdims=True)
                tab_vector[t, 2 * p : 2 * p + 1, :] = jnp.where(prev < 0, 64, prev)
                tab_vector[t, 2 * p + 1 : 2 * p + 2, :] = jnp.where(last < 0, 64, last)
        copy = pltpu.make_async_copy(tab_vector, tab, near_t.at[0])
        copy.start()
        copy.wait()
        for stage in range(3):
            for copy in table_copies(stage):
                copy.wait_send()

    for p in range(3):
        pack(0, p)
    for pool in pools:
        pool[64] = jnp.zeros((max(ROWS), 128), jnp.float32)
    pl.semaphore_wait(barrier, len(partners))
    share_table(0)
    for p in range(3):
        start_a(0, p)
    share_table(1)
    factor_steps(0, 2)
    for t in range(4):
        for p in range(3):
            start_b(t, p)
            if t + 1 < 4:
                wait_send_a(t, p)
                pack(t + 1, p)
                start_a(t + 1, p)
        if t == 0:
            share_table(2)
            factor_steps(2, 4)
        else:
            for p in range(3):
                spread_inverse(2 * t - 1, p)
            if t == 1:
                share_table(3)
                make_tables()
            sum_all(t - 1)
        for p in range(3):
            spread_inverse(2 * t, p)
    sum_all(3)
    for p in range(3):
        spread_inverse(7, p)
        wait_send_a(3, p)
        for t in range(4):
            part = middle[p].at[t, pl.ds(0, 48)]
            pltpu.make_async_copy(part, part, send_b.at[t, p]).wait()
        whole = far[p]
        pltpu.make_async_copy(whole, whole, out_sem.at[p]).wait()


def exchange(where, own, child_tiles, front_matrix):
    f32 = jnp.float32
    scratch = [pltpu.VMEM((8, 4, 2, r, 128), f32) for r in ROWS]
    scratch += [pltpu.VMEM((65, max(ROWS), 128), f32)] * 2
    for _ in range(6):
        scratch += [pltpu.VMEM((SLOTS, r, 128), f32) for r in ROWS]
    scratch += [pltpu.SemaphoreType.DMA((4, 3))] * 6
    scratch += [pltpu.SemaphoreType.DMA((3,))] * 3
    scratch += [pltpu.SemaphoreType.DMA((3, 7, 2)), pltpu.SemaphoreType.DMA((3,))]
    scratch += [pltpu.SemaphoreType.DMA((4,))]
    scratch += [pltpu.VMEM((P_SIZE, P_SIZE), f32)] * 2
    scratch += [pltpu.SemaphoreType.DMA((3, 7)), pltpu.SemaphoreType.DMA((3,))]
    scratch += [pltpu.SemaphoreType.DMA((8,)), pltpu.VMEM((32, 8, 128), jnp.int32)]
    scratch += [pltpu.VMEM((4, 8, 128), jnp.int32), pltpu.SMEM((4, 8, 128), jnp.int32)]
    anywhere = pl.BlockSpec(memory_space=pl.ANY)
    outs = [jax.ShapeDtypeStruct(front_matrix.shape, f32)]
    outs += [jax.ShapeDtypeStruct((4, 4, 16, r, 128), f32) for r in ROWS]
    outs += [jax.ShapeDtypeStruct((4, 64, r, 128), f32) for r in ROWS]
    outs += [jax.ShapeDtypeStruct((P_SIZE, P_SIZE), f32)] * 2
    outs += [jax.ShapeDtypeStruct((8, 4, 4, 8, 128), jnp.int32)]
    results = pl.pallas_call(
        exchange_kernel,
        out_shape=outs,
        in_specs=[pl.BlockSpec(memory_space=pltpu.SMEM)]
        + [pl.BlockSpec(memory_space=pltpu.VMEM)] * 2
        + [anywhere],
        out_specs=[anywhere] * 10,
        scratch_shapes=scratch,
        compiler_params=pltpu.CompilerParams(
            collective_id=1, has_side_effects=True, vmem_limit_bytes=(63 << 20) + (1 << 19)
        ),
        name="exchange",
    )(where, own, child_tiles, front_matrix)
    return results[0], results[7], results[8]


def routing(owner_index, slot_index):
    count = owner_index.shape[0]
    item = lax.broadcasted_iota(jnp.int32, (count, count), 0)
    other = lax.broadcasted_iota(jnp.int32, (count, count), 1)
    same = (owner_index[:, None] == owner_index[None, :]) & (item > other)
    place = owner_index * 2 + jnp.sum(same.astype(jnp.int32), axis=1)
    hit = place[:, None] == lax.broadcasted_iota(jnp.int32, (count, 256), 1)
    where = jnp.sum(jnp.where(hit, lax.broadcasted_iota(jnp.int32, hit.shape, 0), 0), axis=0)
    slots = jnp.sum(jnp.where(hit, slot_index[:, None] + 1, 0), axis=0) - 1
    own = jnp.concatenate([slots.reshape(2, 128), jnp.zeros((6, 128), jnp.int32)], 0)
    return where, own


def line(me, axis):
    return [moved(me, **{axis: step}) for step in (1, 3, 2)]


def file(me):
    near = [moved(me, z=step, k=core) for step, core in ((1, 0), (3, 0), (1, 1), (3, 1), (2, 0), (2, 1))]
    return near + [moved(me, k=1)]


def greet(barrier, partners):
    for to in partners:
        pl.semaphore_signal(barrier, inc=1, device_id=device(to), device_id_type=MESH)


def panel_kernel(
    assembled, rows, columns, low_stage, high_stage, send0, recv0, send1, recv1, send2, recv2, send_x, recv_x, send_y, recv_y, send_z, recv_z
):
    me = position()
    r = me["z"] * 2 + me["k"]
    y, x = me["y"], me["x"]
    c = y * 4 + x
    depth = rows.shape[2]
    half = depth // 2
    low, high = pl.ds(0, half), pl.ds(half, depth - half)
    wide = pl.ds(0, P_SIZE)
    barrier = pltpu.get_barrier_semaphore()
    to_row, to_col = lax.rem(c, 8), 2 * r + c // 8
    from_row, from_col = c // 2, r + 8 * lax.rem(c, 2)
    stays = (to_row == r) & (to_col == c)
    partners = file(me) + line(me, "y") + line(me, "x")
    greet(barrier, partners)

    @pl.when(jnp.logical_not(stays))
    def _():
        pl.semaphore_signal(barrier, inc=1, device_id=(from_row, from_col), device_id_type=MESH)

    pl.semaphore_wait(barrier, len(partners) + jnp.where(stays, 0, 1))

    def remote(source, target, send, recv, to):
        return pltpu.make_async_remote_copy(
            src_ref=source,
            dst_ref=target,
            send_sem=send,
            recv_sem=recv,
            device_id=to,
            device_id_type=MESH,
        )

    steps = (1, 3, 2)

    def root_copies():
        copies = []
        for i, step in enumerate(steps):
            copies.append(
                remote(
                    assembled.at[:, step, low, wide],
                    low_stage,
                    send0.at[0, i],
                    recv0.at[0],
                    device(moved(me, x=step)),
                )
            )
            copies.append(
                remote(
                    assembled.at[step, :, high, wide],
                    high_stage,
                    send0.at[1, i],
                    recv0.at[1],
                    device(moved(me, y=step)),
                )
            )
        return copies

    def low_copies():
        return [
            remote(
                low_stage.at[step],
                rows.at[step, x, low],
                send1.at[0, i],
                recv1.at[0],
                device(moved(me, y=step)),
            )
            for i, step in enumerate(steps)
        ]

    def high_copies():
        return [
            remote(
                high_stage.at[step],
                rows.at[y, step, high],
                send1.at[1, i],
                recv1.at[1],
                device(moved(me, x=step)),
            )
            for i, step in enumerate(steps)
        ]

    at_top, at_side = y == 0, x == 0

    @pl.when(at_top & at_side)
    def _():
        for copy in root_copies():
            copy.start()
        pltpu.make_async_copy(assembled.at[:, 0, low, wide], low_stage, recv0.at[0]).start()
        pltpu.make_async_copy(assembled.at[0, :, high, wide], high_stage, recv0.at[1]).start()

    @pl.when(at_top)
    def _():
        pltpu.make_async_copy(low_stage, low_stage, recv0.at[0]).wait()
        for copy in low_copies():
            copy.start()
        pltpu.make_async_copy(low_stage.at[0], rows.at[0, x, low], recv1.at[0]).start()

    @pl.when(at_side)
    def _():
        pltpu.make_async_copy(high_stage, high_stage, recv0.at[1]).wait()
        for copy in high_copies():
            copy.start()
        pltpu.make_async_copy(high_stage.at[0], rows.at[y, 0, high], recv1.at[1]).start()

    def spread(part, targets, send, recv):
        copies = [
            remote(part, part, send.at[i], recv.at[i], device(to)) for i, to in enumerate(targets)
        ]
        for copy in copies:
            copy.start()
        return copies

    def finish(copies):
        for copy in copies:
            copy.wait()

    mine_low, mine_high = rows.at[y, x, low], rows.at[y, x, high]
    pltpu.make_async_copy(mine_low, mine_low, recv1.at[0]).wait()
    a1 = spread(mine_low, line(me, "x"), send_x.at[0], recv_x.at[0])
    pltpu.make_async_copy(mine_high, mine_high, recv1.at[1]).wait()
    b1 = spread(mine_high, line(me, "y"), send_y.at[0], recv_y.at[0])
    mine = rows.at[y, x]

    @pl.when(jnp.logical_not(stays))
    def _():
        remote(mine, columns.at[to_row], send2, recv2, (to_row, to_col)).start()

    @pl.when(stays)
    def _():
        pltpu.make_async_copy(mine, columns.at[r], recv2).start()

    finish(a1)
    a2 = spread(rows.at[y, :, low], line(me, "y"), send_y.at[1], recv_y.at[1])
    finish(b1)
    b2 = spread(rows.at[:, x, high], line(me, "x"), send_x.at[1], recv_x.at[1])
    held = columns.at[r]
    pltpu.make_async_copy(held, held, recv2).wait()
    z1 = spread(held, file(me), send_z, recv_z)
    finish(z1)
    finish(a2)
    finish(b2)

    @pl.when(jnp.logical_not(stays))
    def _():
        pltpu.make_async_copy(mine, mine, send2).wait()

    @pl.when(at_top & at_side)
    def _():
        for copy in root_copies():
            copy.wait_send()

    @pl.when(at_top)
    def _():
        for copy in low_copies():
            copy.wait_send()

    @pl.when(at_side)
    def _():
        for copy in high_copies():
            copy.wait_send()


def share_panel(assembled):
    depth = assembled.shape[0] // 16
    half = depth // 2
    anywhere = pl.BlockSpec(memory_space=pl.ANY)
    dma = pltpu.SemaphoreType.DMA
    shapes = ((4, 4, depth, P_SIZE), (8, depth, P_SIZE), (4, half, P_SIZE), (4, depth - half, P_SIZE))
    return pl.pallas_call(
        panel_kernel,
        out_shape=[jax.ShapeDtypeStruct(shape, jnp.float32) for shape in shapes],
        in_specs=[anywhere],
        out_specs=[anywhere] * 4,
        scratch_shapes=[
            dma((2, 3)),
            dma((2,)),
            dma((2, 3)),
            dma((2,)),
            dma,
            dma,
            dma((2, 3)),
            dma((2, 3)),
            dma((2, 3)),
            dma((2, 3)),
            dma((7,)),
            dma((7,)),
        ],
        compiler_params=pltpu.CompilerParams(collective_id=3, has_side_effects=True),
        name="share_panel",
    )(assembled.reshape(4, 4, depth, assembled.shape[1]))[:2]


def factor_blocks(work, inverse, first, last):
    n = P_SIZE
    f32 = jnp.float32
    highest = lax.Precision.HIGHEST

    def times(a, b, dims):
        return lax.dot_general(a, b, (dims, ((), ())), precision=highest, preferred_element_type=f32)

    if first == 0:
        block = work[...]
        work[...] = 0.5 * (block + block.T)
        inverse[...] = jnp.zeros((n, n), f32)
    row128 = lax.broadcasted_iota(jnp.int32, (128, 128), 0)
    col128 = lax.broadcasted_iota(jnp.int32, (128, 128), 1)
    row8 = lax.broadcasted_iota(jnp.int32, (8, 1), 0)

    def step(b, carry):
        here = pl.ds(pl.multiple_of(b * 128, 128), 128)
        corner = work[here, here]
        eye = (row128 == col128).astype(f32)
        up = [corner[8 * g : 8 * g + 8] for g in range(16)]
        low = [eye[8 * g : 8 * g + 8] for g in range(16)]
        for j in range(128):
            g, s = j // 8, j % 8
            pivot = up[g][s : s + 1, j : j + 1]
            scale = 1.0 / pivot
            row = up[g][s : s + 1] * scale
            other = low[g][s : s + 1] * scale
            for i in range(g, 16):
                column = up[i][:, j : j + 1]
                if i == g:
                    column = jnp.where(row8 > s, column, 0.0)
                up[i] = up[i] - column * row
                low[i] = low[i] - column * other
        upper = jnp.concatenate(up, 0)
        lower = jnp.concatenate(low, 0)
        pivots = jnp.sum(jnp.where(row128 == col128, upper, 0.0), axis=1, keepdims=True)
        scale = lax.rsqrt(pivots)
        corner_factor = jnp.where(row128 <= col128, upper * scale, 0.0).T
        corner_inverse = jnp.where(row128 >= col128, lower * scale, 0.0)
        below = times(work[:, here], corner_inverse, ((1,), (1,)))
        row = lax.broadcasted_iota(jnp.int32, (n, 128), 0)
        below = jnp.where(row >= b * 128 + 128, below, 0.0)
        work[...] = work[...] - times(below, below, ((1,), (1,)))
        done = lax.broadcasted_iota(jnp.int32, (128, n), 1) < b * 128
        left = times(jnp.where(done, work[here, :], 0.0), inverse[...], ((1,), (0,)))
        inverse[here, :] = -times(corner_inverse, left, ((1,), (0,)))
        inverse[here, here] = corner_inverse
        work[:, here] = below
        work[here, here] = corner_factor
        return carry

    lax.fori_loop(first, last, step, 0)


def split(value):
    high = value.astype(jnp.bfloat16)
    low = (value - high.astype(jnp.float32)).astype(jnp.bfloat16)
    return high, low


def product(a, b):
    def times(x, y):
        return lax.dot_general(x, y, (((1,), (1,)), ((), ())), preferred_element_type=jnp.float32)

    return times(a[0], b[0]) + (times(a[0], b[1]) + times(a[1], b[0]))


def update_kernel(place, rows_raw, columns_raw, inverse, factor, assembled, out, inv_hi, inv_lo, col_hi, col_lo):
    step = pl.program_id(0)
    tile, width = out.shape

    @pl.when(step == 0)
    def _():
        row = lax.broadcasted_iota(jnp.int32, inverse.shape, 0)
        col = lax.broadcasted_iota(jnp.int32, inverse.shape, 1)
        high, low = split(jnp.where(row >= col, inverse[...], 0.0))
        inv_hi[...] = high
        inv_lo[...] = low
        high, low = split(product(split(columns_raw[...]), (high, low)))
        col_hi[...] = high
        col_lo[...] = low

    row_start = place[0] + step * tile
    col_start = place[1]
    panel = product(split(rows_raw[...]), (inv_hi[...], inv_lo[...]))
    change = product(split(panel), (col_hi[...], col_lo[...]))
    row = row_start + lax.broadcasted_iota(jnp.int32, (tile, width), 0)
    col = col_start + lax.broadcasted_iota(jnp.int32, (tile, width), 1)
    out[...] = assembled[...] - jnp.where((row >= col) & (col >= P_SIZE), change, 0.0)

    @pl.when(col_start == 0)
    def _():
        out[:, 0:P_SIZE] = panel

    @pl.when((col_start == 0) & (row_start < P_SIZE))
    def _():
        out[:, 0:P_SIZE] = factor[...]


def update(place, rows_raw, columns_raw, inverse, factor, assembled):
    rows, width = assembled.shape
    tile = 256
    whole = lambda shape: pl.BlockSpec(shape, lambda i: (0, 0))
    bf16 = jnp.bfloat16
    return pl.pallas_call(
        update_kernel,
        grid=(rows // tile,),
        out_shape=jax.ShapeDtypeStruct((rows, width), jnp.float32),
        in_specs=[
            pl.BlockSpec(memory_space=pltpu.SMEM),
            pl.BlockSpec((tile, P_SIZE), lambda i: (i, 0)),
            whole((width, P_SIZE)),
            whole((P_SIZE, P_SIZE)),
            pl.BlockSpec((tile, P_SIZE), lambda i: (jnp.minimum(i, P_SIZE // tile - 1), 0)),
            pl.BlockSpec((tile, width), lambda i: (i, 0)),
        ],
        out_specs=pl.BlockSpec((tile, width), lambda i: (i, 0)),
        scratch_shapes=[
            pltpu.VMEM((P_SIZE, P_SIZE), bf16),
            pltpu.VMEM((P_SIZE, P_SIZE), bf16),
            pltpu.VMEM((width, P_SIZE), bf16),
            pltpu.VMEM((width, P_SIZE), bf16),
        ],
        compiler_params=pltpu.CompilerParams(vmem_limit_bytes=62 << 20),
        name="update",
    )(place, rows_raw, columns_raw, inverse, factor, assembled)


def local(front_matrix, child_tiles, owner_index, slot_index):
    where, own = routing(owner_index, slot_index)
    assembled, inverse, factor = exchange(where, own, child_tiles, front_matrix)
    rows, columns = share_panel(assembled)
    rows_loc, cols_loc = front_matrix.shape
    place = jnp.stack([lax.axis_index("row") * rows_loc, lax.axis_index("col") * cols_loc])
    return update(
        place.astype(jnp.int32),
        rows.reshape(rows_loc, P_SIZE),
        columns.reshape(cols_loc, P_SIZE),
        inverse,
        factor,
        assembled,
    )


def solution(mesh):
    placed = (P("row", "col"), P(("row", "col"), None, None), P(("row", "col")), P(("row", "col")))
    return jax.shard_map(
        local, mesh=mesh, in_specs=placed, out_specs=P("row", "col"), check_vma=False
    )
```
